128 devices in a mesh: gx: 8 (over x_hi, y), gy: 16 (over z, x_lo, core).
Axes of the slice: x: 4 (x_hi: 2, x_lo: 2; x = x_hi * 2 + x_lo), y: 4, z: 4, core: 2. Of those that a mesh axis runs over, the one named last changes fastest.
Arguments:
- action: bfloat16 [36, 32, 256, 2048], P(None, None, 'gx', 'gy'), may hold values from 0 to 8, as said below
- courant: float32 [32], replicated, may hold values from 0.15 to 0.5
- freq_weight: float32 [32], replicated, may hold values from 0.05 to 0.5
- wave_wet: int32 [256, 2048], P('gx', 'gy'), may hold values 0 or 1
- regrid_weights: int32 [4, 256, 2048], P(None, ('gx', 'gy')), may hold values from 2048 to 59392, as said below
- velocity: float32 [2, 20, 256, 2048], P(None, None, ('gx', 'gy')), may hold values from -4 to 4
- tracer: float32 [2, 20, 256, 2048], P(None, None, ('gx', 'gy')), may hold values from 0.5 to 1.5
- profile: float32 [20], replicated, may hold values from 0.3 to 3
- ocean_wet: int32 [256, 2048], P(('gx', 'gy')), may hold values 0 or 1
Outputs:
- action_next: bfloat16 [36, 32, 256, 2048], P(None, None, 'gx', 'gy')
- velocity_next: float32 [2, 20, 256, 2048], P(None, None, ('gx', 'gy'))
- tracer_next: float32 [2, 20, 256, 2048], P(None, None, ('gx', 'gy'))
The draws below stay inside these ranges and needn't reach their ends.
Inputs may be any that keep to these rules, and one draw needn't show every extreme that they name: `action`: Positive. `regrid_weights`: the four weights of each ocean cell sum to 65536.
All inputs are finite; a program needn't handle non-finite values. No bound on the sum of `wave_wet` or of `ocean_wet` on one device may be relied on, other than what follows from the above.
Results may differ from the reference program's by a relative error of at most 0.0035.
Values may be sent and summed in bfloat16 or wider, within the bound.
No kernel may reach another device: no remote copies, remote signals or barrier semaphores. Data moves between devices by JAX's collectives and lax.ppermute only.
A program may use at most 192 MiB of HBM per device.

```python
import math
import jax
import jax.numpy as jnp
from jax import lax

NDIR = 36
NFREQ = 32
LEV = 20
NX = 256
NY = 2048


def draw_action(key, part):
    key = jax.random.fold_in(key, 11)
    amp_key, comp_key = jax.random.split(key)
    log_level = jax.random.uniform(amp_key, (NX, NY), jnp.float32, -1.5, 1.5)
    shape_part = jax.random.uniform(comp_key, (NDIR, NFREQ, NX, NY), jnp.float32, 0.2, 1.0)
    return (jnp.exp(log_level)[None, None] * shape_part).astype(jnp.bfloat16)


def draw_regrid_weights(key, part):
    key = jax.random.fold_in(key, 23)
    leading_three = jax.random.randint(key, (3, NX, NY), 2048, 20481, dtype=jnp.int32)
    remainder = 65536 - jnp.sum(leading_three, axis=0, keepdims=True)
    stacked = jnp.concatenate([leading_three, remainder], axis=0)
    corner = jnp.array([2048, 2048, 2048, 59392], dtype=jnp.int32)
    return stacked.at[:, 0, 0].set(corner)


def touch_ends(values, own_key, low, largest):
    spot = [jax.random.randint(jax.random.fold_in(own_key, axis), (), 0, length) for axis, length in enumerate(values.shape)]
    main_axis = values.shape.index(max(values.shape))
    next_to = spot[:main_axis] + [(spot[main_axis] + 1) % values.shape[main_axis]] + spot[main_axis + 1:]
    return values.at[tuple(spot)].set(low).at[tuple(next_to)].set(largest)


def shard_levels(stream_key, extent, cuts, least, high):
    loudness, own = 1.0, jax.random.fold_in(stream_key, 6)
    for axis_at, parts in cuts:
        heights = jnp.exp(jax.random.uniform(jax.random.fold_in(own, axis_at), (parts,), jnp.float32, least / len(cuts), high / len(cuts)))
        loudness = loudness * jnp.repeat(heights, extent[axis_at] // parts).reshape([-1 if axis == axis_at else 1 for axis in range(len(extent))])
    return loudness


def centred(key, extent, width, limit, cuts=(), held_as=jnp.bfloat16):
    level = shard_levels(key, extent, cuts, -0.22, 0.18) if cuts else 1.0
    values = jax.random.normal(key, extent, jnp.float32) * width * level
    return jnp.minimum(jnp.maximum(values, -limit), limit).astype(held_as)


def setup_inputs(seed: int = 0) -> dict:
    arg_keys = jax.random.split(jax.random.key(seed), 10)
    action = draw_action(jax.random.fold_in(arg_keys[9], 71), 0)
    courant = jnp.clip(jax.random.uniform(arg_keys[1], (NFREQ,), jnp.float32, 0.15, 0.5), 0.15, 0.5)
    freq_weight = jnp.clip(jnp.exp(jax.random.uniform(arg_keys[2], (NFREQ,), jnp.float32, math.log(0.05), math.log(0.5))), 0.05, 0.5)
    wave_wet = touch_ends((jax.random.randint(arg_keys[3], (NX, NY), 0, 10) < 9).astype(jnp.int32), jax.random.fold_in(arg_keys[3], 1), 0, 1)
    regrid_weights = draw_regrid_weights(jax.random.fold_in(arg_keys[9], 71), 0)
    velocity = centred(arg_keys[5], (2, LEV, NX, NY), 0.3, 4.0, ((2, 128),), jnp.float32)
    tracer = jnp.clip(0.5 + 1.0 * jax.random.uniform(arg_keys[6], (2, LEV, NX, NY), jnp.float32) ** shard_levels(arg_keys[6], (2, LEV, NX, NY), ((2, 128),), -0.2, 0.2), 0.5, 1.5)
    profile = jnp.clip(jnp.exp(jax.random.uniform(arg_keys[7], (LEV,), jnp.float32, math.log(0.3), math.log(3.0))), 0.3, 3.0)
    ocean_wet = touch_ends((jax.random.randint(arg_keys[8], (NX, NY), 0, 10) < 9).astype(jnp.int32), jax.random.fold_in(arg_keys[8], 1), 0, 1)
    return dict(action=action, courant=courant, freq_weight=freq_weight, wave_wet=wave_wet, regrid_weights=regrid_weights, velocity=velocity, tracer=tracer, profile=profile, ocean_wet=ocean_wet)


VISCOSITY = 0.1
CORIOLIS = 0.25
COURANT_MAX = 0.4
AGE_RATE = 0.5


def direction_angles(direction_count):
    positions = jnp.arange(direction_count, dtype=jnp.float32)
    return -jnp.pi / 2 + 2.0 * jnp.pi * (positions + 0.5) / direction_count


def stress_table(angles):
    cosine = jnp.cos(angles)
    sine_values = jnp.sin(angles)
    return jnp.stack([cosine * cosine, cosine * sine_values, sine_values * sine_values]) / angles.shape[0]


def upwind_step(center, west_side, east_side, south_side, north_side, speed_x, speed_y):
    return (center - jnp.maximum(speed_x, 0.0) * (center - west_side)
            - jnp.minimum(speed_x, 0.0) * (east_side - center)
            - jnp.maximum(speed_y, 0.0) * (center - south_side)
            - jnp.minimum(speed_y, 0.0) * (north_side - center))


def wave_forces(stress_pad):
    force_x = -((stress_pad[0, 2:, 1:-1] - stress_pad[0, :-2, 1:-1]) / 2.0
                + (stress_pad[1, 1:-1, 2:] - stress_pad[1, 1:-1, :-2]) / 2.0)
    force_y = -((stress_pad[1, 2:, 1:-1] - stress_pad[1, :-2, 1:-1]) / 2.0
                + (stress_pad[2, 1:-1, 2:] - stress_pad[2, 1:-1, :-2]) / 2.0)
    return jnp.stack([force_x, force_y])


def regrid(extended, weights):
    row_count = weights.shape[1]
    col_count = weights.shape[2]
    widened = jnp.pad(extended, ((0, 0), (0, 0), (0, 1)))
    fraction = weights.astype(jnp.float32) / 65536.0
    return (fraction[0] * widened[:, :row_count, :col_count] + fraction[1] * widened[:, :row_count, 1:]
            + fraction[2] * widened[:, 1:, :col_count] + fraction[3] * widened[:, 1:, 1:])


def ocean_step(padded, forcing, profile, wet_int):
    wet_cells = wet_int.astype(jnp.float32)
    center = padded[:, :, 1:-1, 1:-1]
    west_side = padded[:, :, :-2, 1:-1]
    east_side = padded[:, :, 2:, 1:-1]
    south_side = padded[:, :, 1:-1, :-2]
    north_side = padded[:, :, 1:-1, 2:]
    laplace = west_side + east_side + south_side + north_side - 4.0 * center
    weight_level = profile[:, None, None]
    zonal_flow = wet_cells * (center[0] + VISCOSITY * laplace[0] + CORIOLIS * center[1] + weight_level * forcing[0])
    meridional_flow = wet_cells * (center[1] + VISCOSITY * laplace[1] - CORIOLIS * center[0] + weight_level * forcing[1])
    speed_x = jnp.clip(zonal_flow, -COURANT_MAX, COURANT_MAX)
    speed_y = jnp.clip(meridional_flow, -COURANT_MAX, COURANT_MAX)
    advected = upwind_step(center[2:], west_side[2:], east_side[2:], south_side[2:], north_side[2:], speed_x, speed_y)
    concentration = wet_cells * advected[0]
    age_mass = wet_cells * (advected[1] + AGE_RATE * center[2])
    return jnp.stack([zonal_flow, meridional_flow]), jnp.stack([concentration, age_mass])


def reference(action, courant, freq_weight, wave_wet, regrid_weights, velocity, tracer, profile, ocean_wet):
    angles = direction_angles(NDIR)
    wet_wave = wave_wet.astype(jnp.float32)
    trig_table = stress_table(angles)

    def per_direction(inputs):
        slab_data, cosine, sine_values = inputs
        values = slab_data.astype(jnp.float32)
        padded = jnp.pad(values, ((0, 0), (1, 1), (1, 1)))
        speed_x = (courant * cosine)[:, None, None]
        speed_y = (courant * sine_values)[:, None, None]
        advected = upwind_step(values, padded[:, :-2, 1:-1], padded[:, 2:, 1:-1],
                               padded[:, 1:-1, :-2], padded[:, 1:-1, 2:], speed_x, speed_y)
        energy = jnp.sum(freq_weight[:, None, None] * values, axis=0)
        return (advected * wet_wave).astype(jnp.bfloat16), energy

    action_next, energy = lax.map(per_direction, (action, jnp.cos(angles), jnp.sin(angles)))
    stress = jnp.einsum("kd,dxy->kxy", trig_table, energy, precision=lax.Precision.HIGHEST)
    stress_pad = jnp.pad(stress, ((0, 0), (1, 1), (1, 1)))
    forcing = wave_forces(stress_pad)
    ocean_forcing = regrid(jnp.pad(forcing, ((0, 0), (0, 1), (0, 0))), regrid_weights)
    state = jnp.concatenate([velocity, tracer], axis=0)
    padded_state = jnp.pad(state, ((0, 0), (0, 0), (1, 1), (1, 1)))
    velocity_next, tracer_next = ocean_step(padded_state, ocean_forcing, profile, ocean_wet)
    return action_next, velocity_next, tracer_next
```

```python
import functools

import jax
import jax.numpy as jnp
import numpy as np
from jax import lax
from jax.experimental import pallas as pl
from jax.experimental.pallas import tpu as pltpu
from jax.sharding import PartitionSpec as P

VISCOSITY = 0.1
CORIOLIS = 0.25
COURANT_MAX = 0.4
AGE_RATE = 0.5

DIRS = 36
FREQS = 32
GROUP = 3
STEPS = DIRS // GROUP
QUARTER = STEPS // 4
TILE_X = 32
LANES = 128
LEVELS = 20
LEVEL_BLOCK = 2
SEGMENTS = 16
EDGE_ROWS = 4 * LEVELS * SEGMENTS
COLUMN_ROWS = (STEPS // 2) * TILE_X
RING_ROWS = EDGE_ROWS + COLUMN_ROWS

f32 = jnp.float32
bf16 = jnp.bfloat16


def direction_table():
    angles = -np.pi / 2 + 2.0 * np.pi * (np.arange(DIRS) + 0.5) / DIRS
    cosine, sine = np.cos(angles), np.sin(angles)
    table = np.stack(
        [cosine * cosine / DIRS, cosine * sine / DIRS, sine * sine / DIRS,
         np.abs(cosine), np.abs(sine)], axis=1)
    return table.astype(np.float32).reshape(-1)


def from_west(quarter):
    return quarter < 2


def from_south(quarter):
    return quarter in (1, 2)


def for_quarter(step, body):
    for quarter in range(4):
        pl.when(step // QUARTER == quarter)(functools.partial(body, quarter))


def gather_kernel(weight, table, action, velocity, tracer,
                  stress, rows, to_north, to_south, total, picked):
    step = pl.program_id(0)
    lane = lax.broadcasted_iota(jnp.int32, (TILE_X, LANES), 1)

    @pl.when(step == 0)
    def _():
        total[...] = jnp.zeros_like(total)

    @pl.when(step < LEVELS // LEVEL_BLOCK)
    def _():
        for sub in range(LEVEL_BLOCK):
            level = step * LEVEL_BLOCK + sub
            for field in range(4):
                source = (velocity, tracer)[field // 2]
                at = pl.ds(pl.multiple_of((level * 4 + field) * SEGMENTS, SEGMENTS), SEGMENTS)
                first = source[field % 2, sub, pl.ds(0, SEGMENTS, stride=2), :]
                last = source[field % 2, sub, pl.ds(1, SEGMENTS, stride=2), :]
                to_south[at, :] = first.astype(bf16)
                to_north[at, :] = last.astype(bf16)

    def body(quarter):
        row = TILE_X - 1 if from_west(quarter) else 0
        turn = 1 if from_south(quarter) else 0

        def direction(index, column):
            energy = jnp.zeros((TILE_X, LANES), f32)
            for freq in range(FREQS):
                values = action[index, freq].astype(f32)
                energy = energy + weight[freq] * values
                place = index * FREQS + freq
                column = jnp.where(
                    lane == place, pltpu.roll(values, place + turn, 1), column)
                picked[freq:freq + 1, :] = values[row:row + 1, :]
            at = pl.ds(pl.multiple_of(index * FREQS, FREQS), FREQS)
            rows[at, :] = picked[...].astype(bf16)
            base = (step * GROUP + index) * 5
            for part in range(3):
                total[part] += table[base + part] * energy
            return column

        column = lax.fori_loop(0, GROUP, direction, jnp.zeros((TILE_X, LANES), f32))
        if from_south(quarter):
            slot, target = step - QUARTER, to_north
        else:
            slot, target = (step if quarter == 0 else step - 2 * QUARTER), to_south
        at = pl.ds(pl.multiple_of(EDGE_ROWS + slot * TILE_X, TILE_X), TILE_X)
        target[at, :] = column.astype(bf16)

    for_quarter(step, body)

    @pl.when(step == STEPS - 1)
    def _():
        stress[...] = jnp.zeros_like(stress)
        for part in range(3):
            for row in range(2):
                stress[pl.ds(part * 2 + row, SEGMENTS, stride=8), :] = (
                    total[part, pl.ds(row, SEGMENTS, stride=2), :])


def gather(action, weight, table, velocity, tracer):
    state = pl.BlockSpec(
        (2, LEVEL_BLOCK, 32, LANES),
        lambda s: (0, jnp.minimum(s, LEVELS // LEVEL_BLOCK - 1), 0, 0))
    smem = pl.BlockSpec(memory_space=pltpu.SMEM)
    return pl.pallas_call(
        gather_kernel,
        grid=(STEPS,),
        in_specs=[smem, smem,
                  pl.BlockSpec((GROUP, FREQS, TILE_X, LANES), lambda s: (s, 0, 0, 0)),
                  state, state],
        out_specs=[
            pl.BlockSpec((LANES, LANES), lambda s: (0, 0)),
            pl.BlockSpec((GROUP * FREQS, LANES), lambda s: (s, 0)),
            pl.BlockSpec((RING_ROWS, LANES), lambda s: (0, 0)),
            pl.BlockSpec((RING_ROWS, LANES), lambda s: (0, 0)),
        ],
        out_shape=[
            jax.ShapeDtypeStruct((LANES, LANES), f32),
            jax.ShapeDtypeStruct((DIRS * FREQS, LANES), bf16),
            jax.ShapeDtypeStruct((RING_ROWS, LANES), bf16),
            jax.ShapeDtypeStruct((RING_ROWS, LANES), bf16),
        ],
        scratch_shapes=[pltpu.VMEM((3, TILE_X, LANES), f32), pltpu.VMEM((FREQS, LANES), f32)],
        compiler_params=pltpu.CompilerParams(vmem_limit_bytes=40 * 2**20),
        cost_estimate=pl.CostEstimate(
            flops=10**7, bytes_accessed=12 * 10**6, transcendentals=0),
        name="stress_and_edges",
    )(weight, table, action, velocity, tracer)


def advect_kernel(courant, table, inside, action, wet_int, west, east, south, north,
                  moved, fresh, edge):
    step = pl.program_id(0)
    lane = lax.broadcasted_iota(jnp.int32, (TILE_X, LANES), 1)
    line = lax.broadcasted_iota(jnp.int32, (TILE_X, LANES), 0)
    wet = wet_int[...].astype(f32)

    def body(quarter):
        rows = west if from_west(quarter) else east
        columns = south if from_south(quarter) else north
        row = 0 if from_west(quarter) else TILE_X - 1
        column = 0 if from_south(quarter) else LANES - 1
        row_turn = 1 if from_west(quarter) else TILE_X - 1
        column_turn = 1 if from_south(quarter) else LANES - 1
        flag = inside[0] if from_south(quarter) else inside[1]
        edge[...] = columns[...].astype(f32) * flag

        def direction(index, carry):
            at = pl.ds(pl.multiple_of(index * FREQS, FREQS), FREQS)
            fresh[...] = rows[at, :].astype(f32)
            base = (step * GROUP + index) * 5
            size_x, size_y = table[base + 3], table[base + 4]
            for freq in range(FREQS):
                values = action[index, freq].astype(f32)
                speed_x = courant[freq] * size_x
                speed_y = courant[freq] * size_y
                along_x = jnp.where(
                    line == row, fresh[freq:freq + 1, :], pltpu.roll(values, row_turn, 0))
                place = index * FREQS + freq
                along_y = jnp.where(
                    lane == column,
                    pltpu.roll(edge[...], LANES + column - place, 1),
                    pltpu.roll(values, column_turn, 1))
                result = ((1.0 - speed_x - speed_y) * values
                          + speed_x * along_x + speed_y * along_y)
                moved[index, freq] = (wet * result).astype(bf16)
            return carry

        lax.fori_loop(0, GROUP, direction, 0)

    for_quarter(step, body)


def advect(action, courant, table, inside, wet, west, east, south, north):
    smem = pl.BlockSpec(memory_space=pltpu.SMEM)
    half = STEPS // 2
    rows_of = lambda first: pl.BlockSpec(
        (GROUP * FREQS, LANES), lambda s: (jnp.clip(s - first, 0, half - 1), 0))
    skip = EDGE_ROWS // TILE_X
    return pl.pallas_call(
        advect_kernel,
        grid=(STEPS,),
        in_specs=[smem, smem, smem,
                  pl.BlockSpec((GROUP, FREQS, TILE_X, LANES), lambda s: (s, 0, 0, 0)),
                  pl.BlockSpec((TILE_X, LANES), lambda s: (0, 0)),
                  rows_of(0), rows_of(half),
                  pl.BlockSpec((TILE_X, LANES),
                               lambda s: (skip + jnp.clip(s - QUARTER, 0, half - 1), 0)),
                  pl.BlockSpec((TILE_X, LANES),
                               lambda s: (skip + jnp.where(
                                   s < QUARTER, s, jnp.maximum(s - 2 * QUARTER, QUARTER - 1)), 0))],
        out_specs=pl.BlockSpec((GROUP, FREQS, TILE_X, LANES), lambda s: (s, 0, 0, 0)),
        out_shape=jax.ShapeDtypeStruct(action.shape, bf16),
        scratch_shapes=[pltpu.VMEM((FREQS, LANES), f32), pltpu.VMEM((TILE_X, LANES), f32)],
        compiler_params=pltpu.CompilerParams(vmem_limit_bytes=40 * 2**20),
        cost_estimate=pl.CostEstimate(
            flops=5 * 10**7, bytes_accessed=19 * 10**6, transcendentals=0),
        name="advect",
    )(courant, table, inside, action, wet, west, east, south, north)


OCEAN_BLOCK = 5


def ocean_kernel(profile, inside, before, own, after, regrid, wet_int, velocity, tracer,
                 behind, ahead, velocity_next, tracer_next, force):
    shape = (SEGMENTS, LANES)
    lane = lax.broadcasted_iota(jnp.int32, shape, 1)
    segment = lax.broadcasted_iota(jnp.int32, shape, 0)

    def north_of(cells):
        turned = pltpu.roll(cells, LANES - 1, 1)
        following = jnp.where(segment == SEGMENTS - 1, 0.0, pltpu.roll(turned, SEGMENTS - 1, 0))
        return jnp.where(lane == LANES - 1, following, turned)

    def south_of(cells):
        turned = pltpu.roll(cells, 1, 1)
        preceding = jnp.where(segment == 0, 0.0, pltpu.roll(turned, 1, 0))
        return jnp.where(lane == 0, preceding, turned)

    step = pl.program_id(0)

    @pl.when(step == 0)
    def _():
        def stress_row(part, row):
            source, row = ((before, 1) if row < 0 else (own, row) if row < 2 else (after, row - 2))
            return source[pl.ds(part * 2 + row, SEGMENTS, stride=8), :]

        def wave_force(first, second, row):
            across = stress_row(second, row)
            return -((stress_row(first, row + 1) - stress_row(first, row - 1)) / 2.0
                     + (north_of(across) - south_of(across)) / 2.0)

        for part in range(2):
            lines = [wave_force(part, part + 1, row) for row in range(3)]
            lines[2] = lines[2] * inside[2]
            shifted = [north_of(cells) for cells in lines]
            for row in range(2):
                fraction = [
                    regrid[corner, pl.ds(row, SEGMENTS, stride=2), :].astype(f32) / 65536.0
                    for corner in range(4)]
                force[part, row] = (
                    fraction[0] * lines[row] + fraction[1] * shifted[row]
                    + fraction[2] * lines[row + 1] + fraction[3] * shifted[row + 1])

    wet = [wet_int[pl.ds(row, SEGMENTS, stride=2), :].astype(f32) for row in range(2)]

    def level_step(index, carry):
        weight = profile[step * OCEAN_BLOCK + index]

        def around(source, field, place):
            first = source[field, index, pl.ds(0, SEGMENTS, stride=2), :]
            last = source[field, index, pl.ds(1, SEGMENTS, stride=2), :]
            at = pl.ds(pl.multiple_of((index * 4 + place) * SEGMENTS, SEGMENTS), SEGMENTS)
            west = behind[at, :].astype(f32)
            east = ahead[at, :].astype(f32)
            return ((first, west, last, south_of(first), north_of(first)),
                    (last, first, east, south_of(last), north_of(last)))

        zonal, meridional = around(velocity, 0, 0), around(velocity, 1, 1)
        fresh, old = around(tracer, 0, 2), around(tracer, 1, 3)
        for row in range(2):
            def spread(field):
                center, west, east, south, north = field[row]
                return center + VISCOSITY * (west + east + south + north - 4.0 * center)

            u, v = zonal[row][0], meridional[row][0]
            u_next = wet[row] * (spread(zonal) + CORIOLIS * v + weight * force[0, row])
            v_next = wet[row] * (spread(meridional) - CORIOLIS * u + weight * force[1, row])
            speed_x = jnp.clip(u_next, -COURANT_MAX, COURANT_MAX)
            speed_y = jnp.clip(v_next, -COURANT_MAX, COURANT_MAX)
            forward_x, backward_x = jnp.maximum(speed_x, 0.0), jnp.minimum(speed_x, 0.0)
            forward_y, backward_y = jnp.maximum(speed_y, 0.0), jnp.minimum(speed_y, 0.0)

            def upwind(field):
                center, west, east, south, north = field[row]
                return (center - forward_x * (center - west) - backward_x * (east - center)
                        - forward_y * (center - south) - backward_y * (north - center))

            at = pl.ds(row, SEGMENTS, stride=2)
            velocity_next[0, index, at, :] = u_next
            velocity_next[1, index, at, :] = v_next
            tracer_next[0, index, at, :] = wet[row] * upwind(fresh)
            tracer_next[1, index, at, :] = wet[row] * (upwind(old) + AGE_RATE * fresh[row][0])
        return carry

    lax.fori_loop(0, OCEAN_BLOCK, level_step, 0)


def ocean(profile, inside, before, own, after, regrid, wet, velocity, tracer, behind, ahead):
    smem = pl.BlockSpec(memory_space=pltpu.SMEM)
    whole = lambda *shape: pl.BlockSpec(shape, lambda s: (0,) * len(shape))
    state = pl.BlockSpec((2, OCEAN_BLOCK, 32, LANES), lambda s: (0, s, 0, 0))
    edges = pl.BlockSpec((OCEAN_BLOCK * 4 * SEGMENTS, LANES), lambda s: (s, 0))
    return pl.pallas_call(
        ocean_kernel,
        grid=(LEVELS // OCEAN_BLOCK,),
        in_specs=[smem, smem] + [whole(LANES, LANES)] * 3
        + [whole(4, 32, LANES), whole(32, LANES), state, state, edges, edges],
        out_specs=[state, state],
        out_shape=[jax.ShapeDtypeStruct(velocity.shape, f32)] * 2,
        scratch_shapes=[pltpu.VMEM((2, 2, SEGMENTS, LANES), f32)],
        compiler_params=pltpu.CompilerParams(vmem_limit_bytes=40 * 2**20),
        cost_estimate=pl.CostEstimate(
            flops=2 * 10**7, bytes_accessed=4 * 10**6, transcendentals=0),
        name="ocean",
    )(profile, inside, before, own, after, regrid, wet, velocity, tracer, behind, ahead)


def to_segments(cells):
    lead = cells.shape[:-2]
    split = cells.reshape(lead + (2, SEGMENTS, LANES))
    return jnp.swapaxes(split, -3, -2).reshape(lead + (2 * SEGMENTS, LANES))


def from_segments(cells):
    lead = cells.shape[:-2]
    split = cells.reshape(lead + (SEGMENTS, 2, LANES))
    return jnp.swapaxes(split, -3, -2).reshape(lead + (2, SEGMENTS * LANES))


def shift(block, axes, distance):
    count = lax.axis_size(axes)
    return lax.ppermute(
        block, axes,
        [(i, i + distance) for i in range(count) if 0 <= i + distance < count])


def local(action, courant, freq_weight, wave_wet, regrid_weights, velocity, tracer, profile,
          ocean_wet):
    ring = ("gx", "gy")
    table = jnp.asarray(direction_table())
    at_x, at_y = lax.axis_index("gx"), lax.axis_index("gy")
    last_x, last_y = lax.axis_size("gx") - 1, lax.axis_size("gy") - 1
    inside = jnp.stack([
        at_y > 0, at_y < last_y, (at_x < last_x) | (at_y < last_y)]).astype(f32)
    flow, mass = to_segments(velocity), to_segments(tracer)
    stress, rows, to_north, to_south = gather(action, freq_weight, table, flow, mass)
    half = DIRS // 2 * FREQS
    west = shift(rows[:half], "gx", 1)
    east = shift(rows[half:], "gx", -1)
    behind = shift(to_north, ring, 1)
    ahead = shift(to_south, ring, -1)
    own = lax.all_to_all(
        stress.reshape(SEGMENTS, 8, LANES), "gy", split_axis=0, concat_axis=0, tiled=True
    ).reshape(LANES, LANES)
    before = shift(own, ring, 1)
    after = shift(own, ring, -1)
    action_next = advect(
        action, courant, table, inside, wave_wet, west, east, behind, ahead)
    flow_next, mass_next = ocean(
        profile, inside, before, own, after, to_segments(regrid_weights), to_segments(ocean_wet),
        flow, mass, behind, ahead)
    return action_next, from_segments(flow_next), from_segments(mass_next)


def solution(mesh):
    return jax.shard_map(
        local,
        mesh=mesh,
        in_specs=(
            P(None, None, "gx", "gy"),
            P(),
            P(),
            P("gx", "gy"),
            P(None, ("gx", "gy"), None),
            P(None, None, ("gx", "gy"), None),
            P(None, None, ("gx", "gy"), None),
            P(),
            P(("gx", "gy"), None),
        ),
        out_specs=(
            P(None, None, "gx", "gy"),
            P(None, None, ("gx", "gy"), None),
            P(None, None, ("gx", "gy"), None),
        ),
        check_vma=False,
    )
```

```python
import functools

import jax
import jax.numpy as jnp
import numpy as np
from jax import lax
from jax.experimental import pallas as pl
from jax.experimental.pallas import tpu as pltpu
from jax.sharding import PartitionSpec as P

VISCOSITY = 0.1
CORIOLIS = 0.25
COURANT_MAX = 0.4
AGE_RATE = 0.5

DIRS = 36
FREQS = 32
GROUP = 3
STEPS = DIRS // GROUP
QUARTER = STEPS // 4
TILE_X = 32
LANES = 128
LEVELS = 20
LEVEL_BLOCK = 2
SEGMENTS = 16
EDGE_ROWS = 4 * LEVELS * SEGMENTS
COLUMN_ROWS = (STEPS // 2) * TILE_X
RING_ROWS = EDGE_ROWS + COLUMN_ROWS
HALF_ROWS = DIRS // 2 * FREQS
RIM = 16
ROW_ROWS = HALF_ROWS + 3 * RIM
SLOT = 48
VMEM = 56 * 2**20

f32 = jnp.float32
bf16 = jnp.bfloat16


def direction_table():
    angles = -np.pi / 2 + 2.0 * np.pi * (np.arange(DIRS) + 0.5) / DIRS
    cosine, sine = np.cos(angles), np.sin(angles)
    table = np.stack(
        [cosine * cosine / DIRS, cosine * sine / DIRS, sine * sine / DIRS,
         np.abs(cosine), np.abs(sine)], axis=1)
    return table.astype(np.float32).reshape(-1)


def from_west(quarter):
    return quarter < 2


def from_south(quarter):
    return quarter in (1, 2)


def for_quarter(step, body):
    for quarter in range(4):
        pl.when(step // QUARTER == quarter)(functools.partial(body, quarter))


def tiles_of(ref, *index):
    return [ref[(*index, pl.ds(first, 8), slice(None))].astype(f32)
            for first in range(0, TILE_X, 8)]


def thirds(values):
    high = values.astype(bf16)
    rest = values - high.astype(f32)
    middle = rest.astype(bf16)
    return high, middle, (rest - middle.astype(f32)).astype(bf16)


def gather_kernel(weight, table, action, velocity, tracer,
                  stress, to_east, to_west, to_north, to_south, total, picked, column, rim):
    step = pl.program_id(0)
    lane = lax.broadcasted_iota(jnp.int32, (8, LANES), 1)

    @pl.when(step == 0)
    def _():
        total[...] = jnp.zeros_like(total)

    @pl.when(step < LEVELS // LEVEL_BLOCK)
    def _():
        for sub in range(LEVEL_BLOCK):
            level = step * LEVEL_BLOCK + sub
            for field in range(4):
                source = (velocity, tracer)[field // 2]
                at = pl.ds(pl.multiple_of((level * 4 + field) * SEGMENTS, SEGMENTS), SEGMENTS)
                first = source[field % 2, sub, pl.ds(0, SEGMENTS, stride=2), :]
                last = source[field % 2, sub, pl.ds(1, SEGMENTS, stride=2), :]
                to_south[at, :] = first.astype(bf16)
                to_north[at, :] = last.astype(bf16)

    def body(quarter):
        tile, row = (3, 7) if from_west(quarter) else (0, 0)
        turn = 1 if from_south(quarter) else 0
        rows, first_step = (to_east, 0) if from_west(quarter) else (to_west, STEPS // 2)

        def direction(index, columns):
            energy = [jnp.zeros((8, LANES), f32)] * 4
            columns = list(columns)
            for freq in range(FREQS):
                place = index * FREQS + freq
                here = lane == place
                for part, values in enumerate(tiles_of(action, index, freq)):
                    energy[part] = energy[part] + weight[freq] * values
                    columns[part] = jnp.where(
                        here, pltpu.roll(values, place + turn, 1), columns[part])
                    if part == tile:
                        picked[freq:freq + 1, :] = values[row:row + 1, :]
            at = (step - first_step) * (GROUP * FREQS) + index * FREQS
            rows[pl.ds(pl.multiple_of(at, FREQS), FREQS), :] = picked[...].astype(bf16)
            base = (step * GROUP + index) * 5
            for part in range(3):
                for run in range(4):
                    total[part, pl.ds(run * 8, 8), :] += table[base + part] * energy[run]
            return tuple(columns)

        columns = lax.fori_loop(
            0, GROUP, direction, (jnp.zeros((8, LANES), f32),) * 4)
        for run in range(4):
            column[pl.ds(run * 8, 8), :] = columns[run]
        if from_south(quarter):
            slot, target = step - QUARTER, to_north
        else:
            slot, target = (step if quarter == 0 else step - 2 * QUARTER), to_south
        at = pl.ds(pl.multiple_of(EDGE_ROWS + slot * TILE_X, TILE_X), TILE_X)
        target[at, :] = column[...].astype(bf16)

    for_quarter(step, body)

    @pl.when(step == STEPS - 1)
    def _():
        stress[...] = total[...]
        for target, lines in ((to_east, (TILE_X - 1,)), (to_west, (0, 1))):
            rim[...] = jnp.zeros_like(rim)
            for part in range(3):
                for order, line in enumerate(lines):
                    rim[part * 2 + order:part * 2 + order + 1, :] = total[part, line:line + 1, :]
            for order, piece in enumerate(thirds(rim[...])):
                target[pl.ds(HALF_ROWS + order * RIM, RIM), :] = piece


def gather(action, weight, table, velocity, tracer):
    state = pl.BlockSpec(
        (2, LEVEL_BLOCK, 32, LANES),
        lambda s: (0, jnp.minimum(s, LEVELS // LEVEL_BLOCK - 1), 0, 0))
    smem = pl.BlockSpec(memory_space=pltpu.SMEM)
    whole = lambda *shape: pl.BlockSpec(shape, lambda s: (0,) * len(shape))
    return pl.pallas_call(
        gather_kernel,
        grid=(STEPS,),
        in_specs=[smem, smem,
                  pl.BlockSpec((GROUP, FREQS, TILE_X, LANES), lambda s: (s, 0, 0, 0)),
                  state, state],
        out_specs=[whole(3, TILE_X, LANES)] + [whole(ROW_ROWS, LANES)] * 2
        + [whole(RING_ROWS, LANES)] * 2,
        out_shape=[jax.ShapeDtypeStruct((3, TILE_X, LANES), f32)]
        + [jax.ShapeDtypeStruct((ROW_ROWS, LANES), bf16)] * 2
        + [jax.ShapeDtypeStruct((RING_ROWS, LANES), bf16)] * 2,
        scratch_shapes=[pltpu.VMEM((3, TILE_X, LANES), f32), pltpu.VMEM((FREQS, LANES), f32),
                        pltpu.VMEM((TILE_X, LANES), f32), pltpu.VMEM((RIM, LANES), f32)],
        compiler_params=pltpu.CompilerParams(vmem_limit_bytes=VMEM),
        cost_estimate=pl.CostEstimate(
            flops=10**7, bytes_accessed=12 * 10**6, transcendentals=0),
        name="stress_and_edges",
    )(weight, table, action, velocity, tracer)


def pack_kernel(stress, west, east, packed, tall):
    def rim(source):
        pieces = [source[pl.ds(HALF_ROWS + order * RIM, RIM), :].astype(f32)
                  for order in range(3)]
        return pieces[0] + pieces[1] + pieces[2]

    before, after = rim(west), rim(east)
    for part in range(3):
        tall[part, pl.ds(8, TILE_X), :] = stress[part]
        tall[part, 7:8, :] = before[part * 2:part * 2 + 1, :]
        tall[part, 8 + TILE_X:10 + TILE_X, :] = after[part * 2:part * 2 + 2, :]
        for order in range(5):
            packed[pl.ds(part * 5 + order, SEGMENTS, stride=16), :] = (
                tall[part, pl.ds(7 + order, SEGMENTS, stride=2), :])
    packed[pl.ds(15, SEGMENTS, stride=16), :] = jnp.zeros((SEGMENTS, LANES), f32)


def pack(stress, west, east):
    tail = pl.BlockSpec((ROW_ROWS, LANES), lambda: (0, 0))
    return pl.pallas_call(
        pack_kernel,
        in_specs=[pl.BlockSpec((3, TILE_X, LANES), lambda: (0, 0, 0)), tail, tail],
        out_specs=pl.BlockSpec((2 * LANES, LANES), lambda: (0, 0)),
        out_shape=jax.ShapeDtypeStruct((2 * LANES, LANES), f32),
        scratch_shapes=[pltpu.VMEM((3, 48, LANES), f32)],
        name="pack",
    )(stress, west, east)


def advect_kernel(courant, table, inside, action, wet_int, west, east, south, north,
                  moved, shifted, edge):
    step = pl.program_id(0)
    lane = lax.broadcasted_iota(jnp.int32, (8, LANES), 1)
    wet = [wet_int[pl.ds(first, 8), :].astype(f32) for first in range(0, TILE_X, 8)]

    def body(quarter):
        rows = west if from_west(quarter) else east
        columns = south if from_south(quarter) else north
        halo, offset = (7, 7) if from_west(quarter) else (8 + TILE_X, 9)
        column = 0 if from_south(quarter) else LANES - 1
        column_turn = 1 if from_south(quarter) else LANES - 1
        flag = inside[0] if from_south(quarter) else inside[1]
        edge[...] = columns[...].astype(f32) * flag

        def direction(index, carry):
            at = pl.ds(pl.multiple_of(index * FREQS, FREQS), FREQS)
            shifted[pl.ds(halo, FREQS, stride=SLOT), :] = rows[at, :].astype(f32)
            base = (step * GROUP + index) * 5
            size_x, size_y = table[base + 3], table[base + 4]
            for freq in range(FREQS):
                tiles = tiles_of(action, index, freq)
                speed_x = courant[freq] * size_x
                speed_y = courant[freq] * size_y
                stay = 1.0 - speed_x - speed_y
                place = index * FREQS + freq
                for run in range(4):
                    shifted[pl.ds(freq * SLOT + 8 + run * 8, 8), :] = tiles[run]
                for run in range(4):
                    along_x = shifted[pl.ds(freq * SLOT + offset + run * 8, 8), :]
                    along_y = jnp.where(
                        lane == column,
                        pltpu.roll(edge[pl.ds(run * 8, 8), :], LANES + column - place, 1),
                        pltpu.roll(tiles[run], column_turn, 1))
                    result = stay * tiles[run] + speed_x * along_x + speed_y * along_y
                    moved[index, freq, pl.ds(run * 8, 8), :] = (wet[run] * result).astype(bf16)
            return carry

        lax.fori_loop(0, GROUP, direction, 0)

    for_quarter(step, body)


def advect(action, courant, table, inside, wet, west, east, south, north):
    smem = pl.BlockSpec(memory_space=pltpu.SMEM)
    half = STEPS // 2
    rows_of = lambda first: pl.BlockSpec(
        (GROUP * FREQS, LANES), lambda s: (jnp.clip(s - first, 0, half - 1), 0))
    skip = EDGE_ROWS // TILE_X
    return pl.pallas_call(
        advect_kernel,
        grid=(STEPS,),
        in_specs=[smem, smem, smem,
                  pl.BlockSpec((GROUP, FREQS, TILE_X, LANES), lambda s: (s, 0, 0, 0)),
                  pl.BlockSpec((TILE_X, LANES), lambda s: (0, 0)),
                  rows_of(0), rows_of(half),
                  pl.BlockSpec((TILE_X, LANES),
                               lambda s: (skip + jnp.clip(s - QUARTER, 0, half - 1), 0)),
                  pl.BlockSpec((TILE_X, LANES),
                               lambda s: (skip + jnp.where(
                                   s < QUARTER, s, jnp.maximum(s - 2 * QUARTER, QUARTER - 1)), 0))],
        out_specs=pl.BlockSpec((GROUP, FREQS, TILE_X, LANES), lambda s: (s, 0, 0, 0)),
        out_shape=jax.ShapeDtypeStruct(action.shape, bf16),
        scratch_shapes=[pltpu.VMEM((FREQS * SLOT, LANES), f32),
                        pltpu.VMEM((TILE_X, LANES), f32)],
        compiler_params=pltpu.CompilerParams(vmem_limit_bytes=VMEM),
        cost_estimate=pl.CostEstimate(
            flops=5 * 10**7, bytes_accessed=19 * 10**6, transcendentals=0),
        name="advect",
    )(courant, table, inside, action, wet, west, east, south, north)


OCEAN_BLOCK = 5


def ocean_kernel(profile, inside, stress, regrid, wet_int, velocity, tracer,
                 behind, ahead, velocity_next, tracer_next, force):
    shape = (SEGMENTS, LANES)
    lane = lax.broadcasted_iota(jnp.int32, shape, 1)
    segment = lax.broadcasted_iota(jnp.int32, shape, 0)

    def north_of(cells):
        turned = pltpu.roll(cells, LANES - 1, 1)
        following = jnp.where(segment == SEGMENTS - 1, 0.0, pltpu.roll(turned, SEGMENTS - 1, 0))
        return jnp.where(lane == LANES - 1, following, turned)

    def south_of(cells):
        turned = pltpu.roll(cells, 1, 1)
        preceding = jnp.where(segment == 0, 0.0, pltpu.roll(turned, 1, 0))
        return jnp.where(lane == 0, preceding, turned)

    step = pl.program_id(0)

    @pl.when(step == 0)
    def _():
        def stress_row(part, row):
            return stress[pl.ds(part * 5 + row + 1, SEGMENTS, stride=16), :]

        def wave_force(first, second, row):
            across = stress_row(second, row)
            return -((stress_row(first, row + 1) - stress_row(first, row - 1)) / 2.0
                     + (north_of(across) - south_of(across)) / 2.0)

        for part in range(2):
            lines = [wave_force(part, part + 1, row) for row in range(3)]
            lines[2] = lines[2] * inside[2]
            shifted = [north_of(cells) for cells in lines]
            for row in range(2):
                fraction = [
                    regrid[corner, pl.ds(row, SEGMENTS, stride=2), :].astype(f32) / 65536.0
                    for corner in range(4)]
                force[part, row] = (
                    fraction[0] * lines[row] + fraction[1] * shifted[row]
                    + fraction[2] * lines[row + 1] + fraction[3] * shifted[row + 1])

    wet = [wet_int[pl.ds(row, SEGMENTS, stride=2), :].astype(f32) for row in range(2)]

    def level_step(index, carry):
        weight = profile[step * OCEAN_BLOCK + index]

        def around(source, field, place):
            first = source[field, index, pl.ds(0, SEGMENTS, stride=2), :]
            last = source[field, index, pl.ds(1, SEGMENTS, stride=2), :]
            at = pl.ds(pl.multiple_of((index * 4 + place) * SEGMENTS, SEGMENTS), SEGMENTS)
            west = behind[at, :].astype(f32)
            east = ahead[at, :].astype(f32)
            return ((first, west, last, south_of(first), north_of(first)),
                    (last, first, east, south_of(last), north_of(last)))

        zonal, meridional = around(velocity, 0, 0), around(velocity, 1, 1)
        fresh, old = around(tracer, 0, 2), around(tracer, 1, 3)
        for row in range(2):
            def spread(field):
                center, west, east, south, north = field[row]
                return center + VISCOSITY * (west + east + south + north - 4.0 * center)

            u, v = zonal[row][0], meridional[row][0]
            u_next = wet[row] * (spread(zonal) + CORIOLIS * v + weight * force[0, row])
            v_next = wet[row] * (spread(meridional) - CORIOLIS * u + weight * force[1, row])
            speed_x = jnp.clip(u_next, -COURANT_MAX, COURANT_MAX)
            speed_y = jnp.clip(v_next, -COURANT_MAX, COURANT_MAX)
            forward_x, backward_x = jnp.maximum(speed_x, 0.0), jnp.minimum(speed_x, 0.0)
            forward_y, backward_y = jnp.maximum(speed_y, 0.0), jnp.minimum(speed_y, 0.0)

            def upwind(field):
                center, west, east, south, north = field[row]
                return (center - forward_x * (center - west) - backward_x * (east - center)
                        - forward_y * (center - south) - backward_y * (north - center))

            at = pl.ds(row, SEGMENTS, stride=2)
            velocity_next[0, index, at, :] = u_next
            velocity_next[1, index, at, :] = v_next
            tracer_next[0, index, at, :] = wet[row] * upwind(fresh)
            tracer_next[1, index, at, :] = wet[row] * (upwind(old) + AGE_RATE * fresh[row][0])
        return carry

    lax.fori_loop(0, OCEAN_BLOCK, level_step, 0)


def ocean(profile, inside, stress, regrid, wet, velocity, tracer, behind, ahead):
    smem = pl.BlockSpec(memory_space=pltpu.SMEM)
    whole = lambda *shape: pl.BlockSpec(shape, lambda s: (0,) * len(shape))
    state = pl.BlockSpec((2, OCEAN_BLOCK, 32, LANES), lambda s: (0, s, 0, 0))
    edges = pl.BlockSpec((OCEAN_BLOCK * 4 * SEGMENTS, LANES), lambda s: (s, 0))
    return pl.pallas_call(
        ocean_kernel,
        grid=(LEVELS // OCEAN_BLOCK,),
        in_specs=[smem, smem, whole(2 * LANES, LANES), whole(4, 32, LANES), whole(32, LANES),
                  state, state, edges, edges],
        out_specs=[state, state],
        out_shape=[jax.ShapeDtypeStruct(velocity.shape, f32)] * 2,
        scratch_shapes=[pltpu.VMEM((2, 2, SEGMENTS, LANES), f32)],
        compiler_params=pltpu.CompilerParams(vmem_limit_bytes=VMEM),
        cost_estimate=pl.CostEstimate(
            flops=2 * 10**7, bytes_accessed=4 * 10**6, transcendentals=0),
        name="ocean",
    )(profile, inside, stress, regrid, wet, velocity, tracer, behind, ahead)


def to_segments(cells):
    lead = cells.shape[:-2]
    split = cells.reshape(lead + (2, SEGMENTS, LANES))
    return jnp.swapaxes(split, -3, -2).reshape(lead + (2 * SEGMENTS, LANES))


def from_segments(cells):
    lead = cells.shape[:-2]
    split = cells.reshape(lead + (SEGMENTS, 2, LANES))
    return jnp.swapaxes(split, -3, -2).reshape(lead + (2, SEGMENTS * LANES))


def shift(block, axes, distance):
    count = lax.axis_size(axes)
    return lax.ppermute(
        block, axes,
        [(i, i + distance) for i in range(count) if 0 <= i + distance < count])


def local(action, courant, freq_weight, wave_wet, regrid_weights, velocity, tracer, profile,
          ocean_wet):
    ring = ("gx", "gy")
    table = jnp.asarray(direction_table())
    at_x, at_y = lax.axis_index("gx"), lax.axis_index("gy")
    last_x, last_y = lax.axis_size("gx") - 1, lax.axis_size("gy") - 1
    inside = jnp.stack([
        at_y > 0, at_y < last_y, (at_x < last_x) | (at_y < last_y)]).astype(f32)
    flow, mass = to_segments(velocity), to_segments(tracer)
    stress, to_east, to_west, to_north, to_south = gather(
        action, freq_weight, table, flow, mass)
    west = shift(to_east, "gx", 1)
    east = shift(to_west, "gx", -1)
    behind = shift(to_north, ring, 1)
    ahead = shift(to_south, ring, -1)
    strips = lax.all_to_all(
        pack(stress, west, east).reshape(SEGMENTS, 16, LANES), "gy",
        split_axis=0, concat_axis=0, tiled=True).reshape(2 * LANES, LANES)
    action_next = advect(
        action, courant, table, inside, wave_wet, west, east, behind, ahead)
    flow_next, mass_next = ocean(
        profile, inside, strips, to_segments(regrid_weights), to_segments(ocean_wet),
        flow, mass, behind, ahead)
    return action_next, from_segments(flow_next), from_segments(mass_next)


def solution(mesh):
    return jax.shard_map(
        local,
        mesh=mesh,
        in_specs=(
            P(None, None, "gx", "gy"),
            P(),
            P(),
            P("gx", "gy"),
            P(None, ("gx", "gy"), None),
            P(None, None, ("gx", "gy"), None),
            P(None, None, ("gx", "gy"), None),
            P(),
            P(("gx", "gy"), None),
        ),
        out_specs=(
            P(None, None, "gx", "gy"),
            P(None, None, ("gx", "gy"), None),
            P(None, None, ("gx", "gy"), None),
        ),
        check_vma=False,
    )
```

```python
import functools

import jax
import jax.numpy as jnp
import numpy as np
from jax import lax
from jax.experimental import pallas as pl
from jax.experimental.pallas import tpu as pltpu
from jax.sharding import PartitionSpec as P

VISCOSITY = 0.1
CORIOLIS = 0.25
COURANT_MAX = 0.4
AGE_RATE = 0.5

DIRS = 36
FREQS = 32
GROUP = 3
STEPS = DIRS // GROUP
QUARTER = STEPS // 4
TILE_X = 32
LANES = 128
LEVELS = 20
SEGMENTS = 16
EDGE_ROWS = 4 * LEVELS * SEGMENTS
COLUMN_ROWS = (STEPS // 2) * TILE_X
RING_ROWS = EDGE_ROWS + COLUMN_ROWS
HALF_ROWS = DIRS // 2 * FREQS
RIM = 16
ROW_ROWS = HALF_ROWS + 3 * RIM
VMEM = 28 * 2**20
MIDDLE = 48 * 2**20
WIDE = 56 * 2**20

f32 = jnp.float32
bf16 = jnp.bfloat16


def direction_table():
    angles = -np.pi / 2 + 2.0 * np.pi * (np.arange(DIRS) + 0.5) / DIRS
    cosine, sine = np.cos(angles), np.sin(angles)
    return np.stack(
        [cosine * cosine / DIRS, cosine * sine / DIRS, sine * sine / DIRS,
         np.abs(cosine), np.abs(sine)], axis=1).astype(np.float32)


def write_table(table, columns):
    for angle, values in enumerate(direction_table()):
        for place, column in enumerate(columns):
            table[angle * len(columns) + place] = f32(values[column])


def from_west(quarter):
    return quarter < 2


def from_south(quarter):
    return quarter in (1, 2)


def column_slot(quarter, step):
    if from_south(quarter):
        return step - QUARTER
    return step if quarter == 0 else step - 2 * QUARTER


def thirds(values):
    high = values.astype(bf16)
    rest = values - high.astype(f32)
    middle = rest.astype(bf16)
    return high, middle, (rest - middle.astype(f32)).astype(bf16)


def gather_kernel(weight_hbm, action_hbm, velocity_hbm, tracer_hbm,
                  stress, to_east, to_west, to_north, to_south,
                  weight, table, action, velocity, tracer, one_hot, picked, rim, arrived, others):

    def arrival(step):
        slab = pl.ds(step * GROUP, GROUP)
        return pltpu.make_async_copy(action_hbm.at[slab], action.at[slab], arrived.at[step])

    extra = [pltpu.make_async_copy(source, target, others.at[order])
             for order, (source, target) in enumerate(
                 ((weight_hbm, weight), (velocity_hbm, velocity), (tracer_hbm, tracer)))]
    extra[0].start()
    for step in range(STEPS):
        arrival(step).start()
    extra[1].start()
    extra[2].start()
    write_table(table, (0, 1, 2))
    lane = lax.broadcasted_iota(jnp.int32, (16, LANES), 1)
    for place in range(GROUP * FREQS):
        one_hot[pl.ds(place * 16, 16), :] = jnp.where(lane == place, 1.0, 0.0).astype(bf16)
    stress[...] = jnp.zeros_like(stress)
    extra[0].wait()

    def edges(level, carry):
        for field in range(4):
            source = (velocity, tracer)[field // 2]
            at = pl.ds(pl.multiple_of((level * 4 + field) * SEGMENTS, SEGMENTS), SEGMENTS)
            to_south[at, :] = source[field % 2, level, pl.ds(0, SEGMENTS, stride=2), :].astype(bf16)
            to_north[at, :] = source[field % 2, level, pl.ds(1, SEGMENTS, stride=2), :].astype(bf16)
        return carry

    def sweep(quarter, step):
        tile, row = (1, 15) if from_west(quarter) else (0, 0)
        turn = 1 if from_south(quarter) else 0
        rows, first_step = (to_east, 0) if from_west(quarter) else (to_west, STEPS // 2)
        arrival(step).wait()

        def direction(index, columns):
            angle = step * GROUP + index
            energy = [jnp.zeros((16, LANES), f32)] * 2
            columns = list(columns)
            for freq in range(FREQS):
                place = index * FREQS + freq
                hot = one_hot[pl.ds(pl.multiple_of(place * 16, 16), 16), :]
                rolled = pltpu.roll(action[angle, freq], place + turn, 1)
                for half in range(2):
                    own = action[angle, freq, pl.ds(half * 16, 16), :].astype(f32)
                    energy[half] = energy[half] + weight[freq] * own
                    part = freq % 4 * 2 + half
                    columns[part] = columns[part] + rolled[half * 16:half * 16 + 16] * hot
                    if half == tile:
                        picked[freq:freq + 1, :] = own[row:row + 1, :]
            at = (step - first_step) * (GROUP * FREQS) + index * FREQS
            rows[pl.ds(pl.multiple_of(at, FREQS), FREQS), :] = picked[...].astype(bf16)
            for part in range(3):
                for half in range(2):
                    stress[part, pl.ds(half * 16, 16), :] += (
                        table[angle * 3 + part] * energy[half])
            return tuple(columns)

        columns = lax.fori_loop(
            0, GROUP, direction, (jnp.zeros((16, LANES), bf16),) * 8)
        slot, target = column_slot(quarter, step), to_north if from_south(quarter) else to_south
        at = pl.multiple_of(EDGE_ROWS + slot * TILE_X, TILE_X)
        for half in range(2):
            target[pl.ds(at + half * 16, 16), :] = (
                (columns[half] + columns[2 + half]) + (columns[4 + half] + columns[6 + half]))

    for quarter in range(4):
        lax.fori_loop(quarter * QUARTER, (quarter + 1) * QUARTER,
                      lambda step, carry: (sweep(quarter, step), carry)[1], 0)

    extra[1].wait()
    extra[2].wait()
    lax.fori_loop(0, LEVELS, edges, 0)

    for target, lines in ((to_east, (TILE_X - 1,)), (to_west, (0, 1))):
        rim[...] = jnp.zeros_like(rim)
        for part in range(3):
            for order, line in enumerate(lines):
                rim[part * 2 + order:part * 2 + order + 1, :] = stress[part, line:line + 1, :]
        for order, piece in enumerate(thirds(rim[...])):
            target[pl.ds(HALF_ROWS + order * RIM, RIM), :] = piece


VMEM_SPACE = pl.BlockSpec(memory_space=pltpu.VMEM)
SMEM_SPACE = pl.BlockSpec(memory_space=pltpu.SMEM)
HBM_SPACE = pl.BlockSpec(memory_space=pltpu.HBM)


def gather(action, weight, velocity, tracer):
    return pl.pallas_call(
        gather_kernel,
        in_specs=[HBM_SPACE] * 4,
        out_specs=[VMEM_SPACE] * 5,
        out_shape=[jax.ShapeDtypeStruct((3, TILE_X, LANES), f32)]
        + [jax.ShapeDtypeStruct((ROW_ROWS, LANES), bf16)] * 2
        + [jax.ShapeDtypeStruct((RING_ROWS, LANES), bf16)] * 2,
        scratch_shapes=[pltpu.SMEM((FREQS,), f32), pltpu.SMEM((DIRS * 3,), f32),
                        pltpu.VMEM(action.shape, bf16), pltpu.VMEM(velocity.shape, f32),
                        pltpu.VMEM(tracer.shape, f32),
                        pltpu.VMEM((GROUP * FREQS * 16, LANES), bf16),
                        pltpu.VMEM((FREQS, LANES), f32),
                        pltpu.VMEM((RIM, LANES), f32),
                        pltpu.SemaphoreType.DMA((STEPS,)), pltpu.SemaphoreType.DMA((3,))],
        compiler_params=pltpu.CompilerParams(vmem_limit_bytes=WIDE),
        cost_estimate=pl.CostEstimate(
            flops=10**7, bytes_accessed=12 * 10**6, transcendentals=0),
        name="stress_and_edges",
    )(weight, action, velocity, tracer)


def pack_kernel(stress, west, east, packed, tall):
    def rim(source):
        pieces = [source[pl.ds(order * RIM, RIM), :].astype(f32) for order in range(3)]
        return pieces[0] + pieces[1] + pieces[2]

    before, after = rim(west), rim(east)
    for part in range(3):
        tall[part, pl.ds(8, TILE_X), :] = stress[part]
        tall[part, 7:8, :] = before[part * 2:part * 2 + 1, :]
        tall[part, 8 + TILE_X:10 + TILE_X, :] = after[part * 2:part * 2 + 2, :]
        for order in range(5):
            packed[pl.ds(part * 5 + order, SEGMENTS, stride=16), :] = (
                tall[part, pl.ds(7 + order, SEGMENTS, stride=2), :])
    packed[pl.ds(15, SEGMENTS, stride=16), :] = jnp.zeros((SEGMENTS, LANES), f32)


def pack(stress, west, east):
    tail = pl.BlockSpec((3 * RIM, LANES), lambda i: (HALF_ROWS // (3 * RIM), 0))
    return pl.pallas_call(
        pack_kernel,
        grid=(1,),
        in_specs=[pl.BlockSpec((3, TILE_X, LANES), lambda i: (0, 0, 0)), tail, tail],
        out_specs=pl.BlockSpec((2 * LANES, LANES), lambda i: (0, 0)),
        out_shape=jax.ShapeDtypeStruct((2 * LANES, LANES), f32),
        scratch_shapes=[pltpu.VMEM((3, 48, LANES), f32)],
        compiler_params=pltpu.CompilerParams(vmem_limit_bytes=VMEM),
        name="pack",
    )(stress, west, east)


HALVES = (0, 16)
PAIRS = DIRS // 2


def advect_kernel(courant_hbm, action_hbm, wet_hbm, west_hbm, east_hbm, south_hbm, north_hbm,
                  moved_hbm, courant, table, wet_int, west, east, south, north,
                  action, moved, fresh_a, fresh_b, turned_a, turned_b, arrived, others, left):
    lane = lax.broadcasted_iota(jnp.int32, (TILE_X, LANES), 1)
    line = lax.broadcasted_iota(jnp.int32, (TILE_X, LANES), 0)
    at_y, count_y = lax.axis_index("gy"), lax.axis_size("gy")

    def arrival(pair):
        slab = pl.ds(pair * 2, 2)
        return pltpu.make_async_copy(action_hbm.at[slab], action.at[slab], arrived.at[pair])

    def departure(pair):
        slab = pl.ds(pair * 2, 2)
        return pltpu.make_async_copy(moved.at[slab], moved_hbm.at[slab], left.at[pair])

    columns = pl.ds(EDGE_ROWS, COLUMN_ROWS)
    halos = [pltpu.make_async_copy(source, target, others.at[order])
             for order, (source, target) in enumerate((
                 (courant_hbm, courant), (wet_hbm, wet_int),
                 (west_hbm.at[pl.ds(0, HALF_ROWS)], west), (east_hbm.at[pl.ds(0, HALF_ROWS)], east),
                 (south_hbm.at[columns], south), (north_hbm.at[columns], north)))]
    arrival(0).start()
    for copy in halos:
        copy.start()
    for pair in range(1, PAIRS):
        arrival(pair).start()
    write_table(table, (3, 4))
    for copy in halos:
        copy.wait()
    wet = [wet_int[pl.ds(half, 16), :].astype(f32).astype(bf16) for half in HALVES]

    def prepare(angle, fresh, turned):
        westward = angle >= DIRS // 2
        southern = (angle >= DIRS // 4) & (angle < 3 * DIRS // 4)
        step = angle // GROUP
        near = pl.ds(pl.multiple_of(
            jnp.where(westward, angle - DIRS // 2, angle) * FREQS, FREQS), FREQS)
        fresh[...] = jnp.where(westward, east[near, :].astype(f32), west[near, :].astype(f32))
        slot = jnp.where(southern, step - QUARTER,
                         jnp.where(step < QUARTER, step, step - 2 * QUARTER))
        at = pl.ds(pl.multiple_of(slot * TILE_X, TILE_X), TILE_X)
        inside = jnp.where(southern, at_y > 0, at_y < count_y - 1).astype(f32)
        column = (jnp.where(southern, south[at, :].astype(f32), north[at, :].astype(f32))
                  * inside).astype(bf16)
        turn = jnp.where(southern, 1, LANES - 1)
        target = jnp.where(southern, LANES, 2 * LANES - 1) - (angle - step * GROUP) * FREQS
        empty = lane == jnp.where(southern, 0, LANES - 1)
        for freq in range(FREQS):
            own = action[angle, freq]
            turned[pl.ds(freq * TILE_X, TILE_X), :] = jnp.where(
                empty, pltpu.roll(column, target - freq, 1), pltpu.roll(own, turn, 1))
            yield

    def finish(angle, from_west, fresh, turned):
        size_x, size_y = table[angle * 2], table[angle * 2 + 1]
        for freq in range(FREQS):
            speed_x = courant[freq] * size_x
            speed_y = courant[freq] * size_y
            stay = 1.0 - speed_x - speed_y
            own = action[angle, freq].astype(f32)
            along_x = jnp.where(
                line == (0 if from_west else TILE_X - 1), fresh[freq:freq + 1, :],
                pltpu.roll(own, 1 if from_west else TILE_X - 1, 0))
            along_y = turned[pl.ds(freq * TILE_X, TILE_X), :].astype(f32)
            result = (stay * own + speed_x * along_x + speed_y * along_y).astype(bf16)
            for order, half in enumerate(HALVES):
                moved[angle, freq, pl.ds(half, 16), :] = result[half:half + 16] * wet[order]
            yield

    arrival(0).wait()
    for _ in prepare(jnp.int32(0), fresh_a, turned_a):
        pass

    def two_directions(from_west, pair):
        @pl.when(pair < PAIRS - 1)
        def _():
            arrival(pair + 1).wait()

        first = pair * 2
        for _ in zip(finish(first, from_west, fresh_a, turned_a),
                     prepare(first + 1, fresh_b, turned_b)):
            pass
        following = jnp.minimum(first + 2, DIRS - 1)
        for _ in zip(finish(first + 1, from_west, fresh_b, turned_b),
                     prepare(following, fresh_a, turned_a)):
            pass
        departure(pair).start()

    for from_west in (True, False):
        start = 0 if from_west else PAIRS // 2
        lax.fori_loop(start, start + PAIRS // 2,
                      lambda pair, carry: (two_directions(from_west, pair), carry)[1], 0)
    for pair in range(PAIRS):
        departure(pair).wait()


def advect(action, courant, wet, west, east, south, north):
    fresh = pltpu.VMEM((FREQS, LANES), f32)
    turned = pltpu.VMEM((FREQS * TILE_X, LANES), bf16)
    return pl.pallas_call(
        advect_kernel,
        in_specs=[HBM_SPACE] * 7,
        out_specs=HBM_SPACE,
        out_shape=jax.ShapeDtypeStruct(action.shape, bf16),
        scratch_shapes=[pltpu.SMEM((FREQS,), f32), pltpu.SMEM((DIRS * 2,), f32),
                        pltpu.VMEM((TILE_X, LANES), jnp.int32),
                        pltpu.VMEM((HALF_ROWS, LANES), bf16), pltpu.VMEM((HALF_ROWS, LANES), bf16),
                        pltpu.VMEM((COLUMN_ROWS, LANES), bf16),
                        pltpu.VMEM((COLUMN_ROWS, LANES), bf16),
                        pltpu.VMEM(action.shape, bf16), pltpu.VMEM(action.shape, bf16),
                        fresh, fresh, turned, turned,
                        pltpu.SemaphoreType.DMA((PAIRS,)), pltpu.SemaphoreType.DMA((6,)),
                        pltpu.SemaphoreType.DMA((PAIRS,))],
        compiler_params=pltpu.CompilerParams(vmem_limit_bytes=MIDDLE),
        cost_estimate=pl.CostEstimate(
            flops=5 * 10**7, bytes_accessed=19 * 10**6, transcendentals=0),
        name="advect",
    )(courant, action, wet, west, east, south, north)


OCEAN_BLOCK = 5


def ocean_kernel(profile, stress, regrid, wet_int, velocity, tracer,
                 behind, ahead, velocity_next, tracer_next, force):
    shape = (SEGMENTS, LANES)
    lane = lax.broadcasted_iota(jnp.int32, shape, 1)
    segment = lax.broadcasted_iota(jnp.int32, shape, 0)

    def north_of(cells):
        turned = pltpu.roll(cells, LANES - 1, 1)
        following = jnp.where(segment == SEGMENTS - 1, 0.0, pltpu.roll(turned, SEGMENTS - 1, 0))
        return jnp.where(lane == LANES - 1, following, turned)

    def south_of(cells):
        turned = pltpu.roll(cells, 1, 1)
        preceding = jnp.where(segment == 0, 0.0, pltpu.roll(turned, 1, 0))
        return jnp.where(lane == 0, preceding, turned)

    at_end = (lax.axis_index("gx") == lax.axis_size("gx") - 1) & (
        lax.axis_index("gy") == lax.axis_size("gy") - 1)

    if True:
        def stress_row(part, row):
            return stress[pl.ds(part * 5 + row + 1, SEGMENTS, stride=16), :]

        def wave_force(first, second, row):
            across = stress_row(second, row)
            return -((stress_row(first, row + 1) - stress_row(first, row - 1)) / 2.0
                     + (north_of(across) - south_of(across)) / 2.0)

        for part in range(2):
            lines = [wave_force(part, part + 1, row) for row in range(3)]
            lines[2] = jnp.where(at_end, 0.0, lines[2])
            shifted = [north_of(cells) for cells in lines]
            for row in range(2):
                fraction = [
                    regrid[corner, pl.ds(row, SEGMENTS, stride=2), :].astype(f32) / 65536.0
                    for corner in range(4)]
                force[part, row] = (
                    fraction[0] * lines[row] + fraction[1] * shifted[row]
                    + fraction[2] * lines[row + 1] + fraction[3] * shifted[row + 1])

    wet = [wet_int[pl.ds(row, SEGMENTS, stride=2), :].astype(f32) for row in range(2)]

    def level_step(index):
        weight = profile[index]

        def around(source, field, place):
            first = source[field, index, pl.ds(0, SEGMENTS, stride=2), :]
            last = source[field, index, pl.ds(1, SEGMENTS, stride=2), :]
            at = pl.ds(pl.multiple_of((index * 4 + place) * SEGMENTS, SEGMENTS), SEGMENTS)
            west = behind[at, :].astype(f32)
            east = ahead[at, :].astype(f32)
            return ((first, west, last, south_of(first), north_of(first)),
                    (last, first, east, south_of(last), north_of(last)))

        zonal, meridional = around(velocity, 0, 0), around(velocity, 1, 1)
        fresh, old = around(tracer, 0, 2), around(tracer, 1, 3)
        for row in range(2):
            def spread(field):
                center, west, east, south, north = field[row]
                return center + VISCOSITY * (west + east + south + north - 4.0 * center)

            u, v = zonal[row][0], meridional[row][0]
            u_next = wet[row] * (spread(zonal) + CORIOLIS * v + weight * force[0, row])
            v_next = wet[row] * (spread(meridional) - CORIOLIS * u + weight * force[1, row])
            speed_x = jnp.clip(u_next, -COURANT_MAX, COURANT_MAX)
            speed_y = jnp.clip(v_next, -COURANT_MAX, COURANT_MAX)
            forward_x, backward_x = jnp.maximum(speed_x, 0.0), jnp.minimum(speed_x, 0.0)
            forward_y, backward_y = jnp.maximum(speed_y, 0.0), jnp.minimum(speed_y, 0.0)

            def upwind(field):
                center, west, east, south, north = field[row]
                return (center - forward_x * (center - west) - backward_x * (east - center)
                        - forward_y * (center - south) - backward_y * (north - center))

            at = pl.ds(row, SEGMENTS, stride=2)
            velocity_next[0, index, at, :] = u_next
            velocity_next[1, index, at, :] = v_next
            tracer_next[0, index, at, :] = wet[row] * upwind(fresh)
            tracer_next[1, index, at, :] = wet[row] * (upwind(old) + AGE_RATE * fresh[row][0])

    def block(step, carry):
        for sub in range(OCEAN_BLOCK):
            level_step(step * OCEAN_BLOCK + sub)
        return carry

    lax.fori_loop(0, LEVELS // OCEAN_BLOCK, block, 0)


def ocean(profile, stress, regrid, wet, velocity, tracer, behind, ahead):
    return pl.pallas_call(
        ocean_kernel,
        in_specs=[SMEM_SPACE] + [VMEM_SPACE] * 7,
        out_specs=[VMEM_SPACE] * 2,
        out_shape=[jax.ShapeDtypeStruct(velocity.shape, f32)] * 2,
        scratch_shapes=[pltpu.VMEM((2, 2, SEGMENTS, LANES), f32)],
        compiler_params=pltpu.CompilerParams(vmem_limit_bytes=VMEM),
        cost_estimate=pl.CostEstimate(
            flops=2 * 10**7, bytes_accessed=4 * 10**6, transcendentals=0),
        name="ocean",
    )(profile, stress, regrid, wet, velocity, tracer, behind, ahead)


def to_segments(cells):
    lead = cells.shape[:-2]
    split = cells.reshape(lead + (2, SEGMENTS, LANES))
    return jnp.swapaxes(split, -3, -2).reshape(lead + (2 * SEGMENTS, LANES))


def from_segments(cells):
    lead = cells.shape[:-2]
    split = cells.reshape(lead + (SEGMENTS, 2, LANES))
    return jnp.swapaxes(split, -3, -2).reshape(lead + (2, SEGMENTS * LANES))


def shift(block, axes, distance):
    count = lax.axis_size(axes)
    return lax.ppermute(
        block, axes,
        [(i, i + distance) for i in range(count) if 0 <= i + distance < count])


def local(action, courant, freq_weight, wave_wet, regrid_weights, velocity, tracer, profile,
          ocean_wet):
    ring = ("gx", "gy")
    flow, mass = to_segments(velocity), to_segments(tracer)
    stress, to_east, to_west, to_north, to_south = gather(
        action, freq_weight, flow, mass)
    west = shift(to_east, "gx", 1)
    east = shift(to_west, "gx", -1)
    to_north, to_south, west, east = lax.optimization_barrier(
        (to_north, to_south, west, east))
    behind = shift(to_north, ring, 1)
    ahead = shift(to_south, ring, -1)
    strips = lax.all_to_all(
        pack(stress, west, east).reshape(SEGMENTS, 16, LANES), "gy",
        split_axis=0, concat_axis=0, tiled=True).reshape(2 * LANES, LANES)
    action_next = advect(
        action, courant, wave_wet, west, east, behind, ahead)
    flow_next, mass_next = ocean(
        profile, strips, to_segments(regrid_weights), to_segments(ocean_wet),
        flow, mass, behind, ahead)
    return action_next, from_segments(flow_next), from_segments(mass_next)


def solution(mesh):
    return jax.shard_map(
        local,
        mesh=mesh,
        in_specs=(
            P(None, None, "gx", "gy"),
            P(),
            P(),
            P("gx", "gy"),
            P(None, ("gx", "gy"), None),
            P(None, None, ("gx", "gy"), None),
            P(None, None, ("gx", "gy"), None),
            P(),
            P(("gx", "gy"), None),
        ),
        out_specs=(
            P(None, None, "gx", "gy"),
            P(None, None, ("gx", "gy"), None),
            P(None, None, ("gx", "gy"), None),
        ),
        check_vma=False,
    )
```

```python
import functools

import jax
import jax.numpy as jnp
import numpy as np
from jax import lax
from jax.experimental import pallas as pl
from jax.experimental.pallas import tpu as pltpu
from jax.sharding import PartitionSpec as P

VISCOSITY = 0.1
CORIOLIS = 0.25
COURANT_MAX = 0.4
AGE_RATE = 0.5

DIRS = 36
FREQS = 32
GROUP = 3
STEPS = DIRS // GROUP
QUARTER = STEPS // 4
TILE_X = 32
LANES = 128
LEVELS = 20
SEGMENTS = 16
EDGE_ROWS = 4 * LEVELS * SEGMENTS
COLUMN_ROWS = (STEPS // 2) * TILE_X
RING_ROWS = EDGE_ROWS + COLUMN_ROWS
HALF_ROWS = DIRS // 2 * FREQS
RIM = 16
ROW_ROWS = HALF_ROWS + 3 * RIM
VMEM = 28 * 2**20
MIDDLE = 48 * 2**20
WIDE = 56 * 2**20

f32 = jnp.float32
bf16 = jnp.bfloat16


def direction_table():
    angles = -np.pi / 2 + 2.0 * np.pi * (np.arange(DIRS) + 0.5) / DIRS
    cosine, sine = np.cos(angles), np.sin(angles)
    return np.stack(
        [cosine * cosine / DIRS, cosine * sine / DIRS, sine * sine / DIRS,
         np.abs(cosine), np.abs(sine)], axis=1).astype(np.float32)


def write_table(table, columns):
    for angle, values in enumerate(direction_table()):
        for place, column in enumerate(columns):
            table[angle * len(columns) + place] = f32(values[column])


def from_west(quarter):
    return quarter < 2


def from_south(quarter):
    return quarter in (1, 2)


def column_slot(quarter, step):
    if from_south(quarter):
        return step - QUARTER
    return step if quarter == 0 else step - 2 * QUARTER


def thirds(values):
    high = values.astype(bf16)
    rest = values - high.astype(f32)
    middle = rest.astype(bf16)
    return high, middle, (rest - middle.astype(f32)).astype(bf16)


def gather_kernel(weight_hbm, action_hbm, stress, to_east, to_west,
                  weight, table, action, picked, rim, arrived, others):
    def arrival(step):
        slab = pl.ds(step * GROUP, GROUP)
        return pltpu.make_async_copy(action_hbm.at[slab], action.at[slab], arrived.at[step])

    weights_arrive = pltpu.make_async_copy(weight_hbm, weight, others.at[0])
    weights_arrive.start()
    for step in range(STEPS):
        arrival(step).start()
    write_table(table, (0, 1, 2))
    stress[...] = jnp.zeros_like(stress)
    weights_arrive.wait()

    def sweep(west_side, step):
        tile, row = (1, 15) if west_side else (0, 0)
        rows, first_step = (to_east, 0) if west_side else (to_west, STEPS // 2)
        arrival(step).wait()

        def direction(index, carry):
            angle = step * GROUP + index
            energy = [jnp.zeros((16, LANES), f32)] * 4
            for freq in range(FREQS):
                for half in range(2):
                    own = action[angle, freq, pl.ds(half * 16, 16), :].astype(f32)
                    part = freq % 2 * 2 + half
                    energy[part] = energy[part] + weight[freq] * own
                    if half == tile:
                        picked[freq:freq + 1, :] = own[row:row + 1, :]
            at = (step - first_step) * (GROUP * FREQS) + index * FREQS
            rows[pl.ds(pl.multiple_of(at, FREQS), FREQS), :] = picked[...].astype(bf16)
            for half in range(2):
                both = energy[half] + energy[2 + half]
                for part in range(3):
                    stress[part, pl.ds(half * 16, 16), :] += table[angle * 3 + part] * both
            return carry

        lax.fori_loop(0, GROUP, direction, 0)

    for west_side in (True, False):
        start = 0 if west_side else STEPS // 2
        lax.fori_loop(start, start + STEPS // 2,
                      lambda step, carry: (sweep(west_side, step), carry)[1], 0)

    for target, lines in ((to_east, (TILE_X - 1,)), (to_west, (0, 1))):
        rim[...] = jnp.zeros_like(rim)
        for part in range(3):
            for order, line in enumerate(lines):
                rim[part * 2 + order:part * 2 + order + 1, :] = stress[part, line:line + 1, :]
        for order, piece in enumerate(thirds(rim[...])):
            target[pl.ds(HALF_ROWS + order * RIM, RIM), :] = piece


VMEM_SPACE = pl.BlockSpec(memory_space=pltpu.VMEM)
SMEM_SPACE = pl.BlockSpec(memory_space=pltpu.SMEM)
HBM_SPACE = pl.BlockSpec(memory_space=pltpu.HBM)


def gather(action, weight):
    return pl.pallas_call(
        gather_kernel,
        in_specs=[HBM_SPACE] * 2,
        out_specs=[VMEM_SPACE] * 3,
        out_shape=[jax.ShapeDtypeStruct((3, TILE_X, LANES), f32)]
        + [jax.ShapeDtypeStruct((ROW_ROWS, LANES), bf16)] * 2,
        scratch_shapes=[pltpu.SMEM((FREQS,), f32), pltpu.SMEM((DIRS * 3,), f32),
                        pltpu.VMEM(action.shape, bf16), pltpu.VMEM((FREQS, LANES), f32),
                        pltpu.VMEM((RIM, LANES), f32),
                        pltpu.SemaphoreType.DMA((STEPS,)), pltpu.SemaphoreType.DMA((1,))],
        compiler_params=pltpu.CompilerParams(vmem_limit_bytes=WIDE),
        cost_estimate=pl.CostEstimate(
            flops=10**7, bytes_accessed=10**7, transcendentals=0),
        name="stress_and_rows",
    )(weight, action)


def columns_kernel(action_hbm, velocity_hbm, tracer_hbm, to_north, to_south,
                   action, velocity, tracer, one_hot, arrived, others):
    def arrival(step):
        slab = pl.ds(step * GROUP, GROUP)
        return pltpu.make_async_copy(action_hbm.at[slab], action.at[slab], arrived.at[step])

    strips = [pltpu.make_async_copy(source, target, others.at[order])
              for order, (source, target) in enumerate(
                  ((velocity_hbm, velocity), (tracer_hbm, tracer)))]
    for copy in strips:
        copy.start()
    for step in range(STEPS):
        arrival(step).start()
    lane = lax.broadcasted_iota(jnp.int32, (16, LANES), 1)
    for place in range(GROUP * FREQS):
        one_hot[pl.ds(place * 16, 16), :] = jnp.where(lane == place, 1.0, 0.0).astype(bf16)

    for pair, source in enumerate((velocity, tracer)):
        strips[pair].wait()

        def edges(level, carry):
            for field in range(2):
                place = (level * 4 + pair * 2 + field) * SEGMENTS
                at = pl.ds(pl.multiple_of(place, SEGMENTS), SEGMENTS)
                to_south[at, :] = source[field, level, pl.ds(0, SEGMENTS, stride=2), :].astype(bf16)
                to_north[at, :] = source[field, level, pl.ds(1, SEGMENTS, stride=2), :].astype(bf16)
            return carry

        lax.fori_loop(0, LEVELS, edges, 0, unroll=5)

    def sweep(quarter, step):
        turn = 1 if from_south(quarter) else 0
        arrival(step).wait()

        def direction(index, columns):
            angle = step * GROUP + index
            columns = list(columns)
            for freq in range(FREQS):
                place = index * FREQS + freq
                hot = one_hot[pl.ds(pl.multiple_of(place * 16, 16), 16), :]
                rolled = pltpu.roll(action[angle, freq], place + turn, 1)
                for half in range(2):
                    part = freq % 4 * 2 + half
                    columns[part] = columns[part] + rolled[half * 16:half * 16 + 16] * hot
            return tuple(columns)

        columns = lax.fori_loop(
            0, GROUP, direction, (jnp.zeros((16, LANES), bf16),) * 8)
        slot, target = column_slot(quarter, step), to_north if from_south(quarter) else to_south
        at = pl.multiple_of(EDGE_ROWS + slot * TILE_X, TILE_X)
        for half in range(2):
            target[pl.ds(at + half * 16, 16), :] = (
                (columns[half] + columns[2 + half]) + (columns[4 + half] + columns[6 + half]))

    for quarter in range(4):
        lax.fori_loop(quarter * QUARTER, (quarter + 1) * QUARTER,
                      lambda step, carry: (sweep(quarter, step), carry)[1], 0)


def edge_columns(action, velocity, tracer):
    return pl.pallas_call(
        columns_kernel,
        in_specs=[HBM_SPACE] * 3,
        out_specs=[VMEM_SPACE] * 2,
        out_shape=[jax.ShapeDtypeStruct((RING_ROWS, LANES), bf16)] * 2,
        scratch_shapes=[pltpu.VMEM(action.shape, bf16), pltpu.VMEM(velocity.shape, f32),
                        pltpu.VMEM(tracer.shape, f32),
                        pltpu.VMEM((GROUP * FREQS * 16, LANES), bf16),
                        pltpu.SemaphoreType.DMA((STEPS,)), pltpu.SemaphoreType.DMA((2,))],
        compiler_params=pltpu.CompilerParams(vmem_limit_bytes=WIDE),
        cost_estimate=pl.CostEstimate(
            flops=10**7, bytes_accessed=12 * 10**6, transcendentals=0),
        name="ring_edges",
    )(action, velocity, tracer)


def pack_kernel(stress, west, east, packed, tall):
    def rim(source):
        pieces = [source[pl.ds(order * RIM, RIM), :].astype(f32) for order in range(3)]
        return pieces[0] + pieces[1] + pieces[2]

    before, after = rim(west), rim(east)
    for part in range(3):
        tall[part, pl.ds(8, TILE_X), :] = stress[part]
        tall[part, 7:8, :] = before[part * 2:part * 2 + 1, :]
        tall[part, 8 + TILE_X:10 + TILE_X, :] = after[part * 2:part * 2 + 2, :]
        for order in range(5):
            packed[pl.ds(part * 5 + order, SEGMENTS, stride=16), :] = (
                tall[part, pl.ds(7 + order, SEGMENTS, stride=2), :])
    packed[pl.ds(15, SEGMENTS, stride=16), :] = jnp.zeros((SEGMENTS, LANES), f32)


def pack(stress, west, east):
    tail = pl.BlockSpec((3 * RIM, LANES), lambda i: (HALF_ROWS // (3 * RIM), 0))
    return pl.pallas_call(
        pack_kernel,
        grid=(1,),
        in_specs=[pl.BlockSpec((3, TILE_X, LANES), lambda i: (0, 0, 0)), tail, tail],
        out_specs=pl.BlockSpec((2 * LANES, LANES), lambda i: (0, 0)),
        out_shape=jax.ShapeDtypeStruct((2 * LANES, LANES), f32),
        scratch_shapes=[pltpu.VMEM((3, 48, LANES), f32)],
        compiler_params=pltpu.CompilerParams(vmem_limit_bytes=VMEM),
        name="pack",
    )(stress, west, east)


HALVES = (0, 16)
PAIRS = DIRS // 2


def advect_kernel(courant_hbm, action_hbm, wet_hbm, west_hbm, east_hbm, south_hbm, north_hbm,
                  moved_hbm, courant, table, wet_int, west, east, south, north,
                  action, moved, fresh_a, fresh_b, turned_a, turned_b, arrived, others, left):
    lane = lax.broadcasted_iota(jnp.int32, (TILE_X, LANES), 1)
    line = lax.broadcasted_iota(jnp.int32, (TILE_X, LANES), 0)
    at_y, count_y = lax.axis_index("gy"), lax.axis_size("gy")

    def arrival(pair):
        slab = pl.ds(pair * 2, 2)
        return pltpu.make_async_copy(action_hbm.at[slab], action.at[slab], arrived.at[pair])

    def departure(pair):
        slab = pl.ds(pair * 2, 2)
        return pltpu.make_async_copy(moved.at[slab], moved_hbm.at[slab], left.at[pair])

    columns = pl.ds(EDGE_ROWS, COLUMN_ROWS)
    halos = [pltpu.make_async_copy(source, target, others.at[order])
             for order, (source, target) in enumerate((
                 (courant_hbm, courant), (wet_hbm, wet_int),
                 (west_hbm.at[pl.ds(0, HALF_ROWS)], west), (east_hbm.at[pl.ds(0, HALF_ROWS)], east),
                 (south_hbm.at[columns], south), (north_hbm.at[columns], north)))]
    arrival(0).start()
    for copy in halos:
        copy.start()
    for pair in range(1, PAIRS):
        arrival(pair).start()
    write_table(table, (3, 4))
    for copy in halos:
        copy.wait()
    wet = [wet_int[pl.ds(half, 16), :].astype(f32).astype(bf16) for half in HALVES]

    def prepare(angle, fresh, turned):
        westward = angle >= DIRS // 2
        southern = (angle >= DIRS // 4) & (angle < 3 * DIRS // 4)
        step = angle // GROUP
        near = pl.ds(pl.multiple_of(
            jnp.where(westward, angle - DIRS // 2, angle) * FREQS, FREQS), FREQS)
        fresh[...] = jnp.where(westward, east[near, :].astype(f32), west[near, :].astype(f32))
        slot = jnp.where(southern, step - QUARTER,
                         jnp.where(step < QUARTER, step, step - 2 * QUARTER))
        at = pl.ds(pl.multiple_of(slot * TILE_X, TILE_X), TILE_X)
        inside = jnp.where(southern, at_y > 0, at_y < count_y - 1).astype(f32)
        column = (jnp.where(southern, south[at, :].astype(f32), north[at, :].astype(f32))
                  * inside).astype(bf16)
        turn = jnp.where(southern, 1, LANES - 1)
        target = jnp.where(southern, LANES, 2 * LANES - 1) - (angle - step * GROUP) * FREQS
        empty = lane == jnp.where(southern, 0, LANES - 1)
        for freq in range(FREQS):
            own = action[angle, freq]
            turned[pl.ds(freq * TILE_X, TILE_X), :] = jnp.where(
                empty, pltpu.roll(column, target - freq, 1), pltpu.roll(own, turn, 1))
            yield

    def finish(angle, from_west, fresh, turned):
        size_x, size_y = table[angle * 2], table[angle * 2 + 1]
        for freq in range(FREQS):
            speed_x = courant[freq] * size_x
            speed_y = courant[freq] * size_y
            stay = 1.0 - speed_x - speed_y
            own = action[angle, freq].astype(f32)
            along_x = jnp.where(
                line == (0 if from_west else TILE_X - 1), fresh[freq:freq + 1, :],
                pltpu.roll(own, 1 if from_west else TILE_X - 1, 0))
            along_y = turned[pl.ds(freq * TILE_X, TILE_X), :].astype(f32)
            result = (stay * own + speed_x * along_x + speed_y * along_y).astype(bf16)
            for order, half in enumerate(HALVES):
                moved[angle, freq, pl.ds(half, 16), :] = result[half:half + 16] * wet[order]
            yield

    arrival(0).wait()
    for _ in prepare(jnp.int32(0), fresh_a, turned_a):
        pass

    def two_directions(from_west, pair):
        @pl.when(pair < PAIRS - 1)
        def _():
            arrival(pair + 1).wait()

        first = pair * 2
        for _ in zip(finish(first, from_west, fresh_a, turned_a),
                     prepare(first + 1, fresh_b, turned_b)):
            pass
        following = jnp.minimum(first + 2, DIRS - 1)
        for _ in zip(finish(first + 1, from_west, fresh_b, turned_b),
                     prepare(following, fresh_a, turned_a)):
            pass
        departure(pair).start()

    for from_west in (True, False):
        start = 0 if from_west else PAIRS // 2
        lax.fori_loop(start, start + PAIRS // 2,
                      lambda pair, carry: (two_directions(from_west, pair), carry)[1], 0)
    for pair in range(PAIRS):
        departure(pair).wait()


def advect(action, courant, wet, west, east, south, north):
    fresh = pltpu.VMEM((FREQS, LANES), f32)
    turned = pltpu.VMEM((FREQS * TILE_X, LANES), bf16)
    return pl.pallas_call(
        advect_kernel,
        in_specs=[HBM_SPACE] * 7,
        out_specs=HBM_SPACE,
        out_shape=jax.ShapeDtypeStruct(action.shape, bf16),
        scratch_shapes=[pltpu.SMEM((FREQS,), f32), pltpu.SMEM((DIRS * 2,), f32),
                        pltpu.VMEM((TILE_X, LANES), jnp.int32),
                        pltpu.VMEM((HALF_ROWS, LANES), bf16), pltpu.VMEM((HALF_ROWS, LANES), bf16),
                        pltpu.VMEM((COLUMN_ROWS, LANES), bf16),
                        pltpu.VMEM((COLUMN_ROWS, LANES), bf16),
                        pltpu.VMEM(action.shape, bf16), pltpu.VMEM(action.shape, bf16),
                        fresh, fresh, turned, turned,
                        pltpu.SemaphoreType.DMA((PAIRS,)), pltpu.SemaphoreType.DMA((6,)),
                        pltpu.SemaphoreType.DMA((PAIRS,))],
        compiler_params=pltpu.CompilerParams(vmem_limit_bytes=MIDDLE),
        cost_estimate=pl.CostEstimate(
            flops=5 * 10**7, bytes_accessed=19 * 10**6, transcendentals=0),
        name="advect",
    )(courant, action, wet, west, east, south, north)


OCEAN_BLOCK = 5


def ocean_kernel(profile, stress, regrid, wet_int, velocity, tracer,
                 behind, ahead, velocity_next, tracer_next, force):
    shape = (SEGMENTS, LANES)
    lane = lax.broadcasted_iota(jnp.int32, shape, 1)
    segment = lax.broadcasted_iota(jnp.int32, shape, 0)

    def north_of(cells):
        turned = pltpu.roll(cells, LANES - 1, 1)
        following = jnp.where(segment == SEGMENTS - 1, 0.0, pltpu.roll(turned, SEGMENTS - 1, 0))
        return jnp.where(lane == LANES - 1, following, turned)

    def south_of(cells):
        turned = pltpu.roll(cells, 1, 1)
        preceding = jnp.where(segment == 0, 0.0, pltpu.roll(turned, 1, 0))
        return jnp.where(lane == 0, preceding, turned)

    at_end = (lax.axis_index("gx") == lax.axis_size("gx") - 1) & (
        lax.axis_index("gy") == lax.axis_size("gy") - 1)

    if True:
        def stress_row(part, row):
            return stress[pl.ds(part * 5 + row + 1, SEGMENTS, stride=16), :]

        def wave_force(first, second, row):
            across = stress_row(second, row)
            return -((stress_row(first, row + 1) - stress_row(first, row - 1)) / 2.0
                     + (north_of(across) - south_of(across)) / 2.0)

        for part in range(2):
            lines = [wave_force(part, part + 1, row) for row in range(3)]
            lines[2] = jnp.where(at_end, 0.0, lines[2])
            shifted = [north_of(cells) for cells in lines]
            for row in range(2):
                fraction = [
                    regrid[corner, pl.ds(row, SEGMENTS, stride=2), :].astype(f32) / 65536.0
                    for corner in range(4)]
                force[part, row] = (
                    fraction[0] * lines[row] + fraction[1] * shifted[row]
                    + fraction[2] * lines[row + 1] + fraction[3] * shifted[row + 1])

    wet = [wet_int[pl.ds(row, SEGMENTS, stride=2), :].astype(f32) for row in range(2)]

    def level_step(index):
        weight = profile[index]

        def around(source, field, place):
            first = source[field, index, pl.ds(0, SEGMENTS, stride=2), :]
            last = source[field, index, pl.ds(1, SEGMENTS, stride=2), :]
            at = pl.ds(pl.multiple_of((index * 4 + place) * SEGMENTS, SEGMENTS), SEGMENTS)
            west = behind[at, :].astype(f32)
            east = ahead[at, :].astype(f32)
            return ((first, west, last, south_of(first), north_of(first)),
                    (last, first, east, south_of(last), north_of(last)))

        zonal, meridional = around(velocity, 0, 0), around(velocity, 1, 1)
        fresh, old = around(tracer, 0, 2), around(tracer, 1, 3)
        for row in range(2):
            def spread(field):
                center, west, east, south, north = field[row]
                return center + VISCOSITY * (west + east + south + north - 4.0 * center)

            u, v = zonal[row][0], meridional[row][0]
            u_next = wet[row] * (spread(zonal) + CORIOLIS * v + weight * force[0, row])
            v_next = wet[row] * (spread(meridional) - CORIOLIS * u + weight * force[1, row])
            speed_x = jnp.clip(u_next, -COURANT_MAX, COURANT_MAX)
            speed_y = jnp.clip(v_next, -COURANT_MAX, COURANT_MAX)
            forward_x, backward_x = jnp.maximum(speed_x, 0.0), jnp.minimum(speed_x, 0.0)
            forward_y, backward_y = jnp.maximum(speed_y, 0.0), jnp.minimum(speed_y, 0.0)

            def upwind(field):
                center, west, east, south, north = field[row]
                return (center - forward_x * (center - west) - backward_x * (east - center)
                        - forward_y * (center - south) - backward_y * (north - center))

            at = pl.ds(row, SEGMENTS, stride=2)
            velocity_next[0, index, at, :] = u_next
            velocity_next[1, index, at, :] = v_next
            tracer_next[0, index, at, :] = wet[row] * upwind(fresh)
            tracer_next[1, index, at, :] = wet[row] * (upwind(old) + AGE_RATE * fresh[row][0])

    def block(step, carry):
        for sub in range(OCEAN_BLOCK):
            level_step(step * OCEAN_BLOCK + sub)
        return carry

    lax.fori_loop(0, LEVELS // OCEAN_BLOCK, block, 0)


def ocean(profile, stress, regrid, wet, velocity, tracer, behind, ahead):
    return pl.pallas_call(
        ocean_kernel,
        in_specs=[SMEM_SPACE] + [VMEM_SPACE] * 7,
        out_specs=[VMEM_SPACE] * 2,
        out_shape=[jax.ShapeDtypeStruct(velocity.shape, f32)] * 2,
        scratch_shapes=[pltpu.VMEM((2, 2, SEGMENTS, LANES), f32)],
        compiler_params=pltpu.CompilerParams(vmem_limit_bytes=VMEM),
        cost_estimate=pl.CostEstimate(
            flops=2 * 10**7, bytes_accessed=4 * 10**6, transcendentals=0),
        name="ocean",
    )(profile, stress, regrid, wet, velocity, tracer, behind, ahead)


def to_segments(cells):
    lead = cells.shape[:-2]
    split = cells.reshape(lead + (2, SEGMENTS, LANES))
    return jnp.swapaxes(split, -3, -2).reshape(lead + (2 * SEGMENTS, LANES))


def from_segments(cells):
    lead = cells.shape[:-2]
    split = cells.reshape(lead + (SEGMENTS, 2, LANES))
    return jnp.swapaxes(split, -3, -2).reshape(lead + (2, SEGMENTS * LANES))


def shift(block, axes, distance):
    count = lax.axis_size(axes)
    return lax.ppermute(
        block, axes,
        [(i, i + distance) for i in range(count) if 0 <= i + distance < count])


def local(action, courant, freq_weight, wave_wet, regrid_weights, velocity, tracer, profile,
          ocean_wet):
    ring = ("gx", "gy")
    flow, mass = to_segments(velocity), to_segments(tracer)
    stress, to_east, to_west = gather(action, freq_weight)
    west = shift(to_east, "gx", 1)
    east = shift(to_west, "gx", -1)
    to_north, to_south = edge_columns(action, flow, mass)
    to_north, to_south, west, east = lax.optimization_barrier(
        (to_north, to_south, west, east))
    behind = shift(to_north, ring, 1)
    ahead = shift(to_south, ring, -1)
    strips = lax.all_to_all(
        pack(stress, west, east).reshape(SEGMENTS, 16, LANES), "gy",
        split_axis=0, concat_axis=0, tiled=True).reshape(2 * LANES, LANES)
    action_next = advect(
        action, courant, wave_wet, west, east, behind, ahead)
    flow_next, mass_next = ocean(
        profile, strips, to_segments(regrid_weights), to_segments(ocean_wet),
        flow, mass, behind, ahead)
    return action_next, from_segments(flow_next), from_segments(mass_next)


def solution(mesh):
    return jax.shard_map(
        local,
        mesh=mesh,
        in_specs=(
            P(None, None, "gx", "gy"),
            P(),
            P(),
            P("gx", "gy"),
            P(None, ("gx", "gy"), None),
            P(None, None, ("gx", "gy"), None),
            P(None, None, ("gx", "gy"), None),
            P(),
            P(("gx", "gy"), None),
        ),
        out_specs=(
            P(None, None, "gx", "gy"),
            P(None, None, ("gx", "gy"), None),
            P(None, None, ("gx", "gy"), None),
        ),
        check_vma=False,
    )
```

```python
import functools

import jax
import jax.numpy as jnp
import numpy as np
from jax import lax
from jax.experimental import pallas as pl
from jax.experimental.pallas import tpu as pltpu
from jax.sharding import PartitionSpec as P

VISCOSITY = 0.1
CORIOLIS = 0.25
COURANT_MAX = 0.4
AGE_RATE = 0.5

DIRS = 36
FREQS = 32
GROUP = 3
STEPS = DIRS // GROUP
QUARTER = STEPS // 4
TILE_X = 32
LANES = 128
LEVELS = 20
SEGMENTS = 16
EDGE_ROWS = 4 * LEVELS * SEGMENTS
COLUMN_ROWS = (STEPS // 2) * TILE_X
RING_ROWS = EDGE_ROWS + COLUMN_ROWS
HALF_ROWS = DIRS // 2 * FREQS
RIM = 16
ROW_ROWS = HALF_ROWS + 3 * RIM
VMEM = 28 * 2**20
MIDDLE = 48 * 2**20
WIDE = 56 * 2**20

f32 = jnp.float32
bf16 = jnp.bfloat16


def direction_table():
    angles = -np.pi / 2 + 2.0 * np.pi * (np.arange(DIRS) + 0.5) / DIRS
    cosine, sine = np.cos(angles), np.sin(angles)
    return np.stack(
        [cosine * cosine / DIRS, cosine * sine / DIRS, sine * sine / DIRS,
         np.abs(cosine), np.abs(sine)], axis=1).astype(np.float32)


def write_table(table, columns):
    for angle, values in enumerate(direction_table()):
        for place, column in enumerate(columns):
            table[angle * len(columns) + place] = f32(values[column])


def from_west(quarter):
    return quarter < 2


def from_south(quarter):
    return quarter in (1, 2)


def column_slot(quarter, step):
    if from_south(quarter):
        return step - QUARTER
    return step if quarter == 0 else step - 2 * QUARTER


def thirds(values):
    high = values.astype(bf16)
    rest = values - high.astype(f32)
    middle = rest.astype(bf16)
    return high, middle, (rest - middle.astype(f32)).astype(bf16)


def write_one_hot(one_hot):
    lane = lax.broadcasted_iota(jnp.int32, (16, LANES), 1)
    for place in range(GROUP * FREQS):
        one_hot[pl.ds(place * 16, 16), :] = jnp.where(lane == place, 1.0, 0.0).astype(bf16)


def no_columns():
    return (jnp.zeros((16, LANES), bf16),) * 8


def add_column(columns, tile, one_hot, index, freq, turn):
    place = index * FREQS + freq
    hot = one_hot[pl.ds(pl.multiple_of(place * 16, 16), 16), :]
    rolled = pltpu.roll(tile, place + turn, 1)
    for half in range(2):
        part = freq % 4 * 2 + half
        columns[part] = columns[part] + rolled[half * 16:half * 16 + 16] * hot


def put_columns(target, first, columns):
    at = pl.multiple_of(first, TILE_X)
    for half in range(2):
        target[pl.ds(at + half * 16, 16), :] = (
            (columns[half] + columns[2 + half]) + (columns[4 + half] + columns[6 + half]))


def gather_kernel(weight_hbm, action_hbm, stress, to_east, to_west, early,
                  weight, table, action, one_hot, picked, rim, arrived, others):
    def arrival(step):
        slab = pl.ds(step * GROUP, GROUP)
        return pltpu.make_async_copy(action_hbm.at[slab], action.at[slab], arrived.at[step])

    weights_arrive = pltpu.make_async_copy(weight_hbm, weight, others.at[0])
    weights_arrive.start()
    for step in range(STEPS):
        arrival(step).start()
    write_table(table, (0, 1, 2))
    write_one_hot(one_hot)
    stress[...] = jnp.zeros_like(stress)
    weights_arrive.wait()

    def sweep(west_side, step):
        tile, row = (1, 15) if west_side else (0, 0)
        rows, first_step = (to_east, 0) if west_side else (to_west, STEPS // 2)
        turn = jnp.where(step < QUARTER, 0, 1)
        arrival(step).wait()

        def direction(index, columns):
            angle = step * GROUP + index
            energy = [jnp.zeros((16, LANES), f32)] * 4
            columns = list(columns)
            for freq in range(FREQS):
                if west_side:
                    add_column(columns, action[angle, freq], one_hot, index, freq, turn)
                for half in range(2):
                    own = action[angle, freq, pl.ds(half * 16, 16), :].astype(f32)
                    part = freq % 2 * 2 + half
                    energy[part] = energy[part] + weight[freq] * own
                    if half == tile:
                        picked[freq:freq + 1, :] = own[row:row + 1, :]
            at = (step - first_step) * (GROUP * FREQS) + index * FREQS
            rows[pl.ds(pl.multiple_of(at, FREQS), FREQS), :] = picked[...].astype(bf16)
            for half in range(2):
                both = energy[half] + energy[2 + half]
                for part in range(3):
                    stress[part, pl.ds(half * 16, 16), :] += table[angle * 3 + part] * both
            return tuple(columns)

        columns = lax.fori_loop(0, GROUP, direction, no_columns() if west_side else ())
        if west_side:
            put_columns(early, step * TILE_X, columns)

    for west_side in (True, False):
        start = 0 if west_side else STEPS // 2
        lax.fori_loop(start, start + STEPS // 2,
                      lambda step, carry: (sweep(west_side, step), carry)[1], 0)

    for target, lines in ((to_east, (TILE_X - 1,)), (to_west, (0, 1))):
        rim[...] = jnp.zeros_like(rim)
        for part in range(3):
            for order, line in enumerate(lines):
                rim[part * 2 + order:part * 2 + order + 1, :] = stress[part, line:line + 1, :]
        for order, piece in enumerate(thirds(rim[...])):
            target[pl.ds(HALF_ROWS + order * RIM, RIM), :] = piece


VMEM_SPACE = pl.BlockSpec(memory_space=pltpu.VMEM)
SMEM_SPACE = pl.BlockSpec(memory_space=pltpu.SMEM)
HBM_SPACE = pl.BlockSpec(memory_space=pltpu.HBM)


def gather(action, weight):
    return pl.pallas_call(
        gather_kernel,
        in_specs=[HBM_SPACE] * 2,
        out_specs=[VMEM_SPACE] * 4,
        out_shape=[jax.ShapeDtypeStruct((3, TILE_X, LANES), f32)]
        + [jax.ShapeDtypeStruct((ROW_ROWS, LANES), bf16)] * 2
        + [jax.ShapeDtypeStruct((COLUMN_ROWS, LANES), bf16)],
        scratch_shapes=[pltpu.SMEM((FREQS,), f32), pltpu.SMEM((DIRS * 3,), f32),
                        pltpu.VMEM(action.shape, bf16),
                        pltpu.VMEM((GROUP * FREQS * 16, LANES), bf16),
                        pltpu.VMEM((FREQS, LANES), f32),
                        pltpu.VMEM((RIM, LANES), f32),
                        pltpu.SemaphoreType.DMA((STEPS,)), pltpu.SemaphoreType.DMA((1,))],
        compiler_params=pltpu.CompilerParams(vmem_limit_bytes=WIDE),
        cost_estimate=pl.CostEstimate(
            flops=10**7, bytes_accessed=10**7, transcendentals=0),
        name="stress_and_rows",
    )(weight, action)


def columns_kernel(action_hbm, velocity_hbm, tracer_hbm, early_hbm, to_north, to_south,
                   action, velocity, tracer, one_hot, arrived, others):
    half_steps, half_columns = STEPS // 2, COLUMN_ROWS // 2

    def arrival(step):
        return pltpu.make_async_copy(
            action_hbm.at[pl.ds(step * GROUP, GROUP)],
            action.at[pl.ds((step - half_steps) * GROUP, GROUP)], arrived.at[step - half_steps])

    strips = [pltpu.make_async_copy(source, target, others.at[order])
              for order, (source, target) in enumerate((
                  (velocity_hbm, velocity), (tracer_hbm, tracer),
                  (early_hbm.at[pl.ds(0, half_columns)],
                   to_south.at[pl.ds(EDGE_ROWS, half_columns)]),
                  (early_hbm.at[pl.ds(half_columns, half_columns)],
                   to_north.at[pl.ds(EDGE_ROWS, half_columns)])))]
    for step in range(half_steps, STEPS):
        arrival(step).start()
    for copy in strips:
        copy.start()
    write_one_hot(one_hot)

    def sweep(quarter, step):
        turn = 1 if from_south(quarter) else 0
        arrival(step).wait()

        def direction(index, columns):
            columns = list(columns)
            angle = (step - half_steps) * GROUP + index
            for freq in range(FREQS):
                add_column(columns, action[angle, freq], one_hot, index, freq, turn)
            return tuple(columns)

        columns = lax.fori_loop(0, GROUP, direction, no_columns())
        put_columns(to_north if from_south(quarter) else to_south,
                    EDGE_ROWS + column_slot(quarter, step) * TILE_X, columns)

    for quarter in (2, 3):
        lax.fori_loop(quarter * QUARTER, (quarter + 1) * QUARTER,
                      lambda step, carry: (sweep(quarter, step), carry)[1], 0)

    for pair, source in enumerate((velocity, tracer)):
        strips[pair].wait()

        def edges(level, carry):
            for field in range(2):
                place = (level * 4 + pair * 2 + field) * SEGMENTS
                at = pl.ds(pl.multiple_of(place, SEGMENTS), SEGMENTS)
                to_south[at, :] = source[field, level, pl.ds(0, SEGMENTS, stride=2), :].astype(bf16)
                to_north[at, :] = source[field, level, pl.ds(1, SEGMENTS, stride=2), :].astype(bf16)
            return carry

        lax.fori_loop(0, LEVELS, edges, 0, unroll=5)
    strips[2].wait()
    strips[3].wait()


def edge_columns(action, velocity, tracer, early):
    return pl.pallas_call(
        columns_kernel,
        in_specs=[HBM_SPACE] * 4,
        out_specs=[VMEM_SPACE] * 2,
        out_shape=[jax.ShapeDtypeStruct((RING_ROWS, LANES), bf16)] * 2,
        scratch_shapes=[pltpu.VMEM((DIRS // 2,) + action.shape[1:], bf16),
                        pltpu.VMEM(velocity.shape, f32),
                        pltpu.VMEM(tracer.shape, f32),
                        pltpu.VMEM((GROUP * FREQS * 16, LANES), bf16),
                        pltpu.SemaphoreType.DMA((STEPS // 2,)), pltpu.SemaphoreType.DMA((4,))],
        compiler_params=pltpu.CompilerParams(vmem_limit_bytes=WIDE),
        cost_estimate=pl.CostEstimate(
            flops=10**7, bytes_accessed=7 * 10**6, transcendentals=0),
        name="ring_edges",
    )(action, velocity, tracer, early)


def pack_kernel(stress, west, east, packed, tall):
    def rim(source):
        pieces = [source[pl.ds(order * RIM, RIM), :].astype(f32) for order in range(3)]
        return pieces[0] + pieces[1] + pieces[2]

    before, after = rim(west), rim(east)
    for part in range(3):
        tall[part, pl.ds(8, TILE_X), :] = stress[part]
        tall[part, 7:8, :] = before[part * 2:part * 2 + 1, :]
        tall[part, 8 + TILE_X:10 + TILE_X, :] = after[part * 2:part * 2 + 2, :]
        for order in range(5):
            packed[pl.ds(part * 5 + order, SEGMENTS, stride=16), :] = (
                tall[part, pl.ds(7 + order, SEGMENTS, stride=2), :])
    packed[pl.ds(15, SEGMENTS, stride=16), :] = jnp.zeros((SEGMENTS, LANES), f32)


def pack(stress, west, east):
    tail = pl.BlockSpec((3 * RIM, LANES), lambda i: (HALF_ROWS // (3 * RIM), 0))
    return pl.pallas_call(
        pack_kernel,
        grid=(1,),
        in_specs=[pl.BlockSpec((3, TILE_X, LANES), lambda i: (0, 0, 0)), tail, tail],
        out_specs=pl.BlockSpec((2 * LANES, LANES), lambda i: (0, 0)),
        out_shape=jax.ShapeDtypeStruct((2 * LANES, LANES), f32),
        scratch_shapes=[pltpu.VMEM((3, 48, LANES), f32)],
        compiler_params=pltpu.CompilerParams(vmem_limit_bytes=VMEM),
        name="pack",
    )(stress, west, east)


HALVES = (0, 16)
PAIRS = DIRS // 2


def advect_kernel(courant_hbm, action_hbm, wet_hbm, west_hbm, east_hbm, south_hbm, north_hbm,
                  moved_hbm, courant, table, wet_int, west, east, south, north,
                  action, moved, fresh_a, fresh_b, turned_a, turned_b, arrived, others, left):
    lane = lax.broadcasted_iota(jnp.int32, (TILE_X, LANES), 1)
    line = lax.broadcasted_iota(jnp.int32, (TILE_X, LANES), 0)
    at_y, count_y = lax.axis_index("gy"), lax.axis_size("gy")

    def arrival(pair):
        slab = pl.ds(pair * 2, 2)
        return pltpu.make_async_copy(action_hbm.at[slab], action.at[slab], arrived.at[pair])

    def departure(pair):
        slab = pl.ds(pair * 2, 2)
        return pltpu.make_async_copy(moved.at[slab], moved_hbm.at[slab], left.at[pair])

    columns = pl.ds(EDGE_ROWS, COLUMN_ROWS)
    halos = [pltpu.make_async_copy(source, target, others.at[order])
             for order, (source, target) in enumerate((
                 (courant_hbm, courant), (wet_hbm, wet_int),
                 (west_hbm.at[pl.ds(0, HALF_ROWS)], west), (east_hbm.at[pl.ds(0, HALF_ROWS)], east),
                 (south_hbm.at[columns], south), (north_hbm.at[columns], north)))]
    arrival(0).start()
    for copy in halos:
        copy.start()
    for pair in range(1, PAIRS):
        arrival(pair).start()
    write_table(table, (3, 4))
    for copy in halos:
        copy.wait()
    wet = [wet_int[pl.ds(half, 16), :].astype(f32).astype(bf16) for half in HALVES]

    def prepare(angle, fresh, turned):
        westward = angle >= DIRS // 2
        southern = (angle >= DIRS // 4) & (angle < 3 * DIRS // 4)
        step = angle // GROUP
        near = pl.ds(pl.multiple_of(
            jnp.where(westward, angle - DIRS // 2, angle) * FREQS, FREQS), FREQS)
        fresh[...] = jnp.where(westward, east[near, :].astype(f32), west[near, :].astype(f32))
        slot = jnp.where(southern, step - QUARTER,
                         jnp.where(step < QUARTER, step, step - 2 * QUARTER))
        at = pl.ds(pl.multiple_of(slot * TILE_X, TILE_X), TILE_X)
        inside = jnp.where(southern, at_y > 0, at_y < count_y - 1).astype(f32)
        column = (jnp.where(southern, south[at, :].astype(f32), north[at, :].astype(f32))
                  * inside).astype(bf16)
        turn = jnp.where(southern, 1, LANES - 1)
        target = jnp.where(southern, LANES, 2 * LANES - 1) - (angle - step * GROUP) * FREQS
        empty = lane == jnp.where(southern, 0, LANES - 1)
        for freq in range(FREQS):
            own = action[angle, freq]
            turned[pl.ds(freq * TILE_X, TILE_X), :] = jnp.where(
                empty, pltpu.roll(column, target - freq, 1), pltpu.roll(own, turn, 1))
            yield

    def finish(angle, from_west, fresh, turned):
        size_x, size_y = table[angle * 2], table[angle * 2 + 1]
        for freq in range(FREQS):
            speed_x = courant[freq] * size_x
            speed_y = courant[freq] * size_y
            stay = 1.0 - speed_x - speed_y
            own = action[angle, freq].astype(f32)
            along_x = jnp.where(
                line == (0 if from_west else TILE_X - 1), fresh[freq:freq + 1, :],
                pltpu.roll(own, 1 if from_west else TILE_X - 1, 0))
            along_y = turned[pl.ds(freq * TILE_X, TILE_X), :].astype(f32)
            result = (stay * own + speed_x * along_x + speed_y * along_y).astype(bf16)
            for order, half in enumerate(HALVES):
                moved[angle, freq, pl.ds(half, 16), :] = result[half:half + 16] * wet[order]
            yield

    arrival(0).wait()
    for _ in prepare(jnp.int32(0), fresh_a, turned_a):
        pass

    def two_directions(from_west, pair):
        @pl.when(pair < PAIRS - 1)
        def _():
            arrival(pair + 1).wait()

        first = pair * 2
        for _ in zip(finish(first, from_west, fresh_a, turned_a),
                     prepare(first + 1, fresh_b, turned_b)):
            pass
        following = jnp.minimum(first + 2, DIRS - 1)
        for _ in zip(finish(first + 1, from_west, fresh_b, turned_b),
                     prepare(following, fresh_a, turned_a)):
            pass
        departure(pair).start()

    for from_west in (True, False):
        start = 0 if from_west else PAIRS // 2
        lax.fori_loop(start, start + PAIRS // 2,
                      lambda pair, carry: (two_directions(from_west, pair), carry)[1], 0)
    for pair in range(PAIRS):
        departure(pair).wait()


def advect(action, courant, wet, west, east, south, north):
    fresh = pltpu.VMEM((FREQS, LANES), f32)
    turned = pltpu.VMEM((FREQS * TILE_X, LANES), bf16)
    return pl.pallas_call(
        advect_kernel,
        in_specs=[HBM_SPACE] * 7,
        out_specs=HBM_SPACE,
        out_shape=jax.ShapeDtypeStruct(action.shape, bf16),
        scratch_shapes=[pltpu.SMEM((FREQS,), f32), pltpu.SMEM((DIRS * 2,), f32),
                        pltpu.VMEM((TILE_X, LANES), jnp.int32),
                        pltpu.VMEM((HALF_ROWS, LANES), bf16), pltpu.VMEM((HALF_ROWS, LANES), bf16),
                        pltpu.VMEM((COLUMN_ROWS, LANES), bf16),
                        pltpu.VMEM((COLUMN_ROWS, LANES), bf16),
                        pltpu.VMEM(action.shape, bf16), pltpu.VMEM(action.shape, bf16),
                        fresh, fresh, turned, turned,
                        pltpu.SemaphoreType.DMA((PAIRS,)), pltpu.SemaphoreType.DMA((6,)),
                        pltpu.SemaphoreType.DMA((PAIRS,))],
        compiler_params=pltpu.CompilerParams(vmem_limit_bytes=MIDDLE),
        cost_estimate=pl.CostEstimate(
            flops=5 * 10**7, bytes_accessed=19 * 10**6, transcendentals=0),
        name="advect",
    )(courant, action, wet, west, east, south, north)


OCEAN_BLOCK = 5


def ocean_kernel(profile, stress, regrid, wet_int, velocity, tracer,
                 behind, ahead, velocity_next, tracer_next, force):
    shape = (SEGMENTS, LANES)
    lane = lax.broadcasted_iota(jnp.int32, shape, 1)
    segment = lax.broadcasted_iota(jnp.int32, shape, 0)

    def north_of(cells):
        turned = pltpu.roll(cells, LANES - 1, 1)
        following = jnp.where(segment == SEGMENTS - 1, 0.0, pltpu.roll(turned, SEGMENTS - 1, 0))
        return jnp.where(lane == LANES - 1, following, turned)

    def south_of(cells):
        turned = pltpu.roll(cells, 1, 1)
        preceding = jnp.where(segment == 0, 0.0, pltpu.roll(turned, 1, 0))
        return jnp.where(lane == 0, preceding, turned)

    at_end = (lax.axis_index("gx") == lax.axis_size("gx") - 1) & (
        lax.axis_index("gy") == lax.axis_size("gy") - 1)

    if True:
        def stress_row(part, row):
            return stress[pl.ds(part * 5 + row + 1, SEGMENTS, stride=16), :]

        def wave_force(first, second, row):
            across = stress_row(second, row)
            return -((stress_row(first, row + 1) - stress_row(first, row - 1)) / 2.0
                     + (north_of(across) - south_of(across)) / 2.0)

        for part in range(2):
            lines = [wave_force(part, part + 1, row) for row in range(3)]
            lines[2] = jnp.where(at_end, 0.0, lines[2])
            shifted = [north_of(cells) for cells in lines]
            for row in range(2):
                fraction = [
                    regrid[corner, pl.ds(row, SEGMENTS, stride=2), :].astype(f32) / 65536.0
                    for corner in range(4)]
                force[part, row] = (
                    fraction[0] * lines[row] + fraction[1] * shifted[row]
                    + fraction[2] * lines[row + 1] + fraction[3] * shifted[row + 1])

    wet = [wet_int[pl.ds(row, SEGMENTS, stride=2), :].astype(f32) for row in range(2)]

    def level_step(index):
        weight = profile[index]

        def around(source, field, place):
            first = source[field, index, pl.ds(0, SEGMENTS, stride=2), :]
            last = source[field, index, pl.ds(1, SEGMENTS, stride=2), :]
            at = pl.ds(pl.multiple_of((index * 4 + place) * SEGMENTS, SEGMENTS), SEGMENTS)
            west = behind[at, :].astype(f32)
            east = ahead[at, :].astype(f32)
            return ((first, west, last, south_of(first), north_of(first)),
                    (last, first, east, south_of(last), north_of(last)))

        zonal, meridional = around(velocity, 0, 0), around(velocity, 1, 1)
        fresh, old = around(tracer, 0, 2), around(tracer, 1, 3)
        for row in range(2):
            def spread(field):
                center, west, east, south, north = field[row]
                return center + VISCOSITY * (west + east + south + north - 4.0 * center)

            u, v = zonal[row][0], meridional[row][0]
            u_next = wet[row] * (spread(zonal) + CORIOLIS * v + weight * force[0, row])
            v_next = wet[row] * (spread(meridional) - CORIOLIS * u + weight * force[1, row])
            speed_x = jnp.clip(u_next, -COURANT_MAX, COURANT_MAX)
            speed_y = jnp.clip(v_next, -COURANT_MAX, COURANT_MAX)
            forward_x, backward_x = jnp.maximum(speed_x, 0.0), jnp.minimum(speed_x, 0.0)
            forward_y, backward_y = jnp.maximum(speed_y, 0.0), jnp.minimum(speed_y, 0.0)

            def upwind(field):
                center, west, east, south, north = field[row]
                return (center - forward_x * (center - west) - backward_x * (east - center)
                        - forward_y * (center - south) - backward_y * (north - center))

            at = pl.ds(row, SEGMENTS, stride=2)
            velocity_next[0, index, at, :] = u_next
            velocity_next[1, index, at, :] = v_next
            tracer_next[0, index, at, :] = wet[row] * upwind(fresh)
            tracer_next[1, index, at, :] = wet[row] * (upwind(old) + AGE_RATE * fresh[row][0])

    def block(step, carry):
        for sub in range(OCEAN_BLOCK):
            level_step(step * OCEAN_BLOCK + sub)
        return carry

    lax.fori_loop(0, LEVELS // OCEAN_BLOCK, block, 0)


def ocean(profile, stress, regrid, wet, velocity, tracer, behind, ahead):
    return pl.pallas_call(
        ocean_kernel,
        in_specs=[SMEM_SPACE] + [VMEM_SPACE] * 7,
        out_specs=[VMEM_SPACE] * 2,
        out_shape=[jax.ShapeDtypeStruct(velocity.shape, f32)] * 2,
        scratch_shapes=[pltpu.VMEM((2, 2, SEGMENTS, LANES), f32)],
        compiler_params=pltpu.CompilerParams(vmem_limit_bytes=VMEM),
        cost_estimate=pl.CostEstimate(
            flops=2 * 10**7, bytes_accessed=4 * 10**6, transcendentals=0),
        name="ocean",
    )(profile, stress, regrid, wet, velocity, tracer, behind, ahead)


def to_segments(cells):
    lead = cells.shape[:-2]
    split = cells.reshape(lead + (2, SEGMENTS, LANES))
    return jnp.swapaxes(split, -3, -2).reshape(lead + (2 * SEGMENTS, LANES))


def from_segments(cells):
    lead = cells.shape[:-2]
    split = cells.reshape(lead + (SEGMENTS, 2, LANES))
    return jnp.swapaxes(split, -3, -2).reshape(lead + (2, SEGMENTS * LANES))


def shift(block, axes, distance):
    count = lax.axis_size(axes)
    return lax.ppermute(
        block, axes,
        [(i, i + distance) for i in range(count) if 0 <= i + distance < count])


def local(action, courant, freq_weight, wave_wet, regrid_weights, velocity, tracer, profile,
          ocean_wet):
    ring = ("gx", "gy")
    flow, mass = to_segments(velocity), to_segments(tracer)
    stress, to_east, to_west, early = gather(action, freq_weight)
    west = shift(to_east, "gx", 1)
    east = shift(to_west, "gx", -1)
    to_north, to_south = edge_columns(action, flow, mass, early)
    to_north, to_south, west, east = lax.optimization_barrier(
        (to_north, to_south, west, east))
    behind = shift(to_north, ring, 1)
    ahead = shift(to_south, ring, -1)
    strips = lax.all_to_all(
        pack(stress, west, east).reshape(SEGMENTS, 16, LANES), "gy",
        split_axis=0, concat_axis=0, tiled=True).reshape(2 * LANES, LANES)
    action_next = advect(
        action, courant, wave_wet, west, east, behind, ahead)
    flow_next, mass_next = ocean(
        profile, strips, to_segments(regrid_weights), to_segments(ocean_wet),
        flow, mass, behind, ahead)
    return action_next, from_segments(flow_next), from_segments(mass_next)


def solution(mesh):
    return jax.shard_map(
        local,
        mesh=mesh,
        in_specs=(
            P(None, None, "gx", "gy"),
            P(),
            P(),
            P("gx", "gy"),
            P(None, ("gx", "gy"), None),
            P(None, None, ("gx", "gy"), None),
            P(None, None, ("gx", "gy"), None),
            P(),
            P(("gx", "gy"), None),
        ),
        out_specs=(
            P(None, None, "gx", "gy"),
            P(None, None, ("gx", "gy"), None),
            P(None, None, ("gx", "gy"), None),
        ),
        check_vma=False,
    )
```

```python
import functools

import jax
import jax.numpy as jnp
import numpy as np
from jax import lax
from jax.experimental import pallas as pl
from jax.experimental.pallas import tpu as pltpu
from jax.sharding import PartitionSpec as P

VISCOSITY = 0.1
CORIOLIS = 0.25
COURANT_MAX = 0.4
AGE_RATE = 0.5

DIRS = 36
FREQS = 32
GROUP = 3
STEPS = DIRS // GROUP
QUARTER = STEPS // 4
TILE_X = 32
LANES = 128
LEVELS = 20
SEGMENTS = 16
EDGE_ROWS = 4 * LEVELS * SEGMENTS
COLUMN_ROWS = (STEPS // 2) * TILE_X
RING_ROWS = EDGE_ROWS + COLUMN_ROWS
HALF_ROWS = DIRS // 2 * FREQS
RIM = 16
ROW_ROWS = HALF_ROWS + 3 * RIM
VMEM = 28 * 2**20
MIDDLE = 48 * 2**20
WIDE = 56 * 2**20

f32 = jnp.float32
bf16 = jnp.bfloat16


def direction_table():
    angles = -np.pi / 2 + 2.0 * np.pi * (np.arange(DIRS) + 0.5) / DIRS
    cosine, sine = np.cos(angles), np.sin(angles)
    return np.stack(
        [cosine * cosine / DIRS, cosine * sine / DIRS, sine * sine / DIRS,
         np.abs(cosine), np.abs(sine)], axis=1).astype(np.float32)


def write_table(table, columns):
    for angle, values in enumerate(direction_table()):
        for place, column in enumerate(columns):
            table[angle * len(columns) + place] = f32(values[column])


def from_west(quarter):
    return quarter < 2


def from_south(quarter):
    return quarter in (1, 2)


def column_slot(quarter, step):
    if from_south(quarter):
        return step - QUARTER
    return step if quarter == 0 else step - 2 * QUARTER


def thirds(values):
    high = values.astype(bf16)
    rest = values - high.astype(f32)
    middle = rest.astype(bf16)
    return high, middle, (rest - middle.astype(f32)).astype(bf16)


def write_one_hot(one_hot):
    lane = lax.broadcasted_iota(jnp.int32, (16, LANES), 1)
    for place in range(GROUP * FREQS):
        one_hot[pl.ds(place * 16, 16), :] = jnp.where(lane == place, 1.0, 0.0).astype(bf16)


def no_columns():
    return (jnp.zeros((16, LANES), bf16),) * 8


def add_column(columns, tile, one_hot, index, freq, turn):
    place = index * FREQS + freq
    hot = one_hot[pl.ds(pl.multiple_of(place * 16, 16), 16), :]
    rolled = pltpu.roll(tile, place + turn, 1)
    for half in range(2):
        part = freq % 4 * 2 + half
        columns[part] = columns[part] + rolled[half * 16:half * 16 + 16] * hot


def put_columns(target, first, columns):
    at = pl.multiple_of(first, TILE_X)
    for half in range(2):
        target[pl.ds(at + half * 16, 16), :] = (
            (columns[half] + columns[2 + half]) + (columns[4 + half] + columns[6 + half]))


def gather_kernel(weight_hbm, action_hbm, stress, to_east, to_west, early,
                  weight, table, action, one_hot, picked, rim, arrived, others):
    def arrival(step):
        slab = pl.ds(step * GROUP, GROUP)
        return pltpu.make_async_copy(action_hbm.at[slab], action.at[slab], arrived.at[step])

    weights_arrive = pltpu.make_async_copy(weight_hbm, weight, others.at[0])
    weights_arrive.start()
    for step in range(STEPS):
        arrival(step).start()
    write_table(table, (0, 1, 2))
    write_one_hot(one_hot)
    stress[...] = jnp.zeros_like(stress)
    weights_arrive.wait()

    def sweep(west_side, step):
        tile, row = (1, 15) if west_side else (0, 0)
        rows, first_step = (to_east, 0) if west_side else (to_west, STEPS // 2)
        turn = jnp.where(step < QUARTER, 0, 1)
        arrival(step).wait()

        def direction(index, columns):
            angle = step * GROUP + index
            energy = [jnp.zeros((16, LANES), f32)] * 4
            columns = list(columns)
            for freq in range(FREQS):
                if west_side:
                    add_column(columns, action[angle, freq], one_hot, index, freq, turn)
                for half in range(2):
                    own = action[angle, freq, pl.ds(half * 16, 16), :].astype(f32)
                    part = freq % 2 * 2 + half
                    energy[part] = energy[part] + weight[freq] * own
                    if half == tile:
                        picked[freq:freq + 1, :] = own[row:row + 1, :]
            at = (step - first_step) * (GROUP * FREQS) + index * FREQS
            rows[pl.ds(pl.multiple_of(at, FREQS), FREQS), :] = picked[...].astype(bf16)
            for half in range(2):
                both = energy[half] + energy[2 + half]
                for part in range(3):
                    stress[part, pl.ds(half * 16, 16), :] += table[angle * 3 + part] * both
            return tuple(columns)

        columns = lax.fori_loop(0, GROUP, direction, no_columns() if west_side else ())
        if west_side:
            put_columns(early, step * TILE_X, columns)

    for west_side in (True, False):
        start = 0 if west_side else STEPS // 2
        lax.fori_loop(start, start + STEPS // 2,
                      lambda step, carry: (sweep(west_side, step), carry)[1], 0)

    for target, lines in ((to_east, (TILE_X - 1,)), (to_west, (0, 1))):
        rim[...] = jnp.zeros_like(rim)
        for part in range(3):
            for order, line in enumerate(lines):
                rim[part * 2 + order:part * 2 + order + 1, :] = stress[part, line:line + 1, :]
        for order, piece in enumerate(thirds(rim[...])):
            target[pl.ds(HALF_ROWS + order * RIM, RIM), :] = piece


VMEM_SPACE = pl.BlockSpec(memory_space=pltpu.VMEM)
SMEM_SPACE = pl.BlockSpec(memory_space=pltpu.SMEM)
HBM_SPACE = pl.BlockSpec(memory_space=pltpu.HBM)


def gather(action, weight):
    return pl.pallas_call(
        gather_kernel,
        in_specs=[HBM_SPACE] * 2,
        out_specs=[VMEM_SPACE] * 4,
        out_shape=[jax.ShapeDtypeStruct((3, TILE_X, LANES), f32)]
        + [jax.ShapeDtypeStruct((ROW_ROWS, LANES), bf16)] * 2
        + [jax.ShapeDtypeStruct((COLUMN_ROWS, LANES), bf16)],
        scratch_shapes=[pltpu.SMEM((FREQS,), f32), pltpu.SMEM((DIRS * 3,), f32),
                        pltpu.VMEM(action.shape, bf16),
                        pltpu.VMEM((GROUP * FREQS * 16, LANES), bf16),
                        pltpu.VMEM((FREQS, LANES), f32),
                        pltpu.VMEM((RIM, LANES), f32),
                        pltpu.SemaphoreType.DMA((STEPS,)), pltpu.SemaphoreType.DMA((1,))],
        compiler_params=pltpu.CompilerParams(vmem_limit_bytes=WIDE),
        cost_estimate=pl.CostEstimate(
            flops=10**7, bytes_accessed=10**7, transcendentals=0),
        name="stress_and_rows",
    )(weight, action)


def columns_kernel(action_hbm, velocity_hbm, tracer_hbm, early_hbm, to_north, to_south,
                   action, velocity, tracer, one_hot, arrived, others):
    half_steps, half_columns = STEPS // 2, COLUMN_ROWS // 2

    def arrival(step):
        return pltpu.make_async_copy(
            action_hbm.at[pl.ds(step * GROUP, GROUP)],
            action.at[pl.ds((step - half_steps) * GROUP, GROUP)], arrived.at[step - half_steps])

    strips = [pltpu.make_async_copy(source, target, others.at[order])
              for order, (source, target) in enumerate((
                  (velocity_hbm, velocity), (tracer_hbm, tracer),
                  (early_hbm.at[pl.ds(0, half_columns)],
                   to_south.at[pl.ds(EDGE_ROWS, half_columns)]),
                  (early_hbm.at[pl.ds(half_columns, half_columns)],
                   to_north.at[pl.ds(EDGE_ROWS, half_columns)])))]
    for step in range(half_steps, STEPS):
        arrival(step).start()
    for copy in strips:
        copy.start()
    write_one_hot(one_hot)

    def sweep(quarter, step):
        turn = 1 if from_south(quarter) else 0
        arrival(step).wait()

        def direction(index, columns):
            columns = list(columns)
            angle = (step - half_steps) * GROUP + index
            for freq in range(FREQS):
                add_column(columns, action[angle, freq], one_hot, index, freq, turn)
            return tuple(columns)

        columns = lax.fori_loop(0, GROUP, direction, no_columns())
        put_columns(to_north if from_south(quarter) else to_south,
                    EDGE_ROWS + column_slot(quarter, step) * TILE_X, columns)

    for quarter in (2, 3):
        lax.fori_loop(quarter * QUARTER, (quarter + 1) * QUARTER,
                      lambda step, carry: (sweep(quarter, step), carry)[1], 0)

    for pair, source in enumerate((velocity, tracer)):
        strips[pair].wait()

        def edges(level, carry):
            for field in range(2):
                place = (level * 4 + pair * 2 + field) * SEGMENTS
                at = pl.ds(pl.multiple_of(place, SEGMENTS), SEGMENTS)
                to_south[at, :] = source[field, level, pl.ds(0, SEGMENTS, stride=2), :].astype(bf16)
                to_north[at, :] = source[field, level, pl.ds(1, SEGMENTS, stride=2), :].astype(bf16)
            return carry

        lax.fori_loop(0, LEVELS, edges, 0, unroll=5)
    strips[2].wait()
    strips[3].wait()


def edge_columns(action, velocity, tracer, early):
    return pl.pallas_call(
        columns_kernel,
        in_specs=[HBM_SPACE] * 4,
        out_specs=[VMEM_SPACE] * 2,
        out_shape=[jax.ShapeDtypeStruct((RING_ROWS, LANES), bf16)] * 2,
        scratch_shapes=[pltpu.VMEM((DIRS // 2,) + action.shape[1:], bf16),
                        pltpu.VMEM(velocity.shape, f32),
                        pltpu.VMEM(tracer.shape, f32),
                        pltpu.VMEM((GROUP * FREQS * 16, LANES), bf16),
                        pltpu.SemaphoreType.DMA((STEPS // 2,)), pltpu.SemaphoreType.DMA((4,))],
        compiler_params=pltpu.CompilerParams(vmem_limit_bytes=WIDE),
        cost_estimate=pl.CostEstimate(
            flops=10**7, bytes_accessed=7 * 10**6, transcendentals=0),
        name="ring_edges",
    )(action, velocity, tracer, early)


def pack_kernel(stress, west, east, packed, tall):
    def rim(source):
        pieces = [source[pl.ds(order * RIM, RIM), :].astype(f32) for order in range(3)]
        return pieces[0] + pieces[1] + pieces[2]

    before, after = rim(west), rim(east)
    for part in range(3):
        tall[part, pl.ds(8, TILE_X), :] = stress[part]
        tall[part, 7:8, :] = before[part * 2:part * 2 + 1, :]
        tall[part, 8 + TILE_X:10 + TILE_X, :] = after[part * 2:part * 2 + 2, :]
        for order in range(5):
            packed[pl.ds(part * 5 + order, SEGMENTS, stride=16), :] = (
                tall[part, pl.ds(7 + order, SEGMENTS, stride=2), :])
    packed[pl.ds(15, SEGMENTS, stride=16), :] = jnp.zeros((SEGMENTS, LANES), f32)


def pack(stress, west, east):
    tail = pl.BlockSpec((3 * RIM, LANES), lambda i: (HALF_ROWS // (3 * RIM), 0))
    return pl.pallas_call(
        pack_kernel,
        grid=(1,),
        in_specs=[pl.BlockSpec((3, TILE_X, LANES), lambda i: (0, 0, 0)), tail, tail],
        out_specs=pl.BlockSpec((2 * LANES, LANES), lambda i: (0, 0)),
        out_shape=jax.ShapeDtypeStruct((2 * LANES, LANES), f32),
        scratch_shapes=[pltpu.VMEM((3, 48, LANES), f32)],
        compiler_params=pltpu.CompilerParams(vmem_limit_bytes=VMEM),
        name="pack",
    )(stress, west, east)


HALVES = (0, 16)
PAIRS = DIRS // 2


def advect_kernel(courant_hbm, action_hbm, wet_hbm, west_hbm, east_hbm, south_hbm, north_hbm,
                  moved_hbm, courant, table, wet_int, west, east, south, north,
                  action, moved, fresh_a, fresh_b, turned_a, turned_b, arrived, others, left):
    lane = lax.broadcasted_iota(jnp.int32, (TILE_X, LANES), 1)
    line = lax.broadcasted_iota(jnp.int32, (TILE_X, LANES), 0)
    at_y, count_y = lax.axis_index("gy"), lax.axis_size("gy")

    def arrival(pair):
        slab = pl.ds(pair * 2, 2)
        return pltpu.make_async_copy(action_hbm.at[slab], action.at[slab], arrived.at[pair])

    def departure(pair):
        slab = pl.ds(pair * 2, 2)
        return pltpu.make_async_copy(moved.at[slab], moved_hbm.at[slab], left.at[pair])

    columns = pl.ds(EDGE_ROWS, COLUMN_ROWS)
    halos = [pltpu.make_async_copy(source, target, others.at[order])
             for order, (source, target) in enumerate((
                 (courant_hbm, courant), (wet_hbm, wet_int),
                 (west_hbm.at[pl.ds(0, HALF_ROWS)], west), (east_hbm.at[pl.ds(0, HALF_ROWS)], east),
                 (south_hbm.at[columns], south), (north_hbm.at[columns], north)))]
    arrival(0).start()
    for copy in halos:
        copy.start()
    for pair in range(1, PAIRS):
        arrival(pair).start()
    write_table(table, (3, 4))
    for copy in halos:
        copy.wait()
    wet = [wet_int[pl.ds(half, 16), :].astype(f32).astype(bf16) for half in HALVES]

    def prepare(angle, fresh, turned):
        westward = angle >= DIRS // 2
        southern = (angle >= DIRS // 4) & (angle < 3 * DIRS // 4)
        step = angle // GROUP
        near = pl.ds(pl.multiple_of(
            jnp.where(westward, angle - DIRS // 2, angle) * FREQS, FREQS), FREQS)
        fresh[...] = jnp.where(westward, east[near, :].astype(f32), west[near, :].astype(f32))
        slot = jnp.where(southern, step - QUARTER,
                         jnp.where(step < QUARTER, step, step - 2 * QUARTER))
        at = pl.ds(pl.multiple_of(slot * TILE_X, TILE_X), TILE_X)
        inside = jnp.where(southern, at_y > 0, at_y < count_y - 1).astype(f32)
        column = (jnp.where(southern, south[at, :].astype(f32), north[at, :].astype(f32))
                  * inside).astype(bf16)
        turn = jnp.where(southern, 1, LANES - 1)
        target = jnp.where(southern, LANES, 2 * LANES - 1) - (angle - step * GROUP) * FREQS
        empty = lane == jnp.where(southern, 0, LANES - 1)
        for freq in range(FREQS):
            own = action[angle, freq]
            turned[pl.ds(freq * TILE_X, TILE_X), :] = jnp.where(
                empty, pltpu.roll(column, target - freq, 1), pltpu.roll(own, turn, 1))
            yield

    def finish(angle, from_west, fresh, turned):
        size_x, size_y = table[angle * 2], table[angle * 2 + 1]
        for freq in range(FREQS):
            speed_x = courant[freq] * size_x
            speed_y = courant[freq] * size_y
            stay = 1.0 - speed_x - speed_y
            own = action[angle, freq].astype(f32)
            along_x = jnp.where(
                line == (0 if from_west else TILE_X - 1), fresh[freq:freq + 1, :],
                pltpu.roll(own, 1 if from_west else TILE_X - 1, 0))
            along_y = turned[pl.ds(freq * TILE_X, TILE_X), :].astype(f32)
            result = (stay * own + speed_x * along_x + speed_y * along_y).astype(bf16)
            for order, half in enumerate(HALVES):
                moved[angle, freq, pl.ds(half, 16), :] = result[half:half + 16] * wet[order]
            yield

    arrival(0).wait()
    for _ in prepare(jnp.int32(0), fresh_a, turned_a):
        pass

    def two_directions(from_west, pair):
        @pl.when(pair < PAIRS - 1)
        def _():
            arrival(pair + 1).wait()

        first = pair * 2
        for _ in zip(finish(first, from_west, fresh_a, turned_a),
                     prepare(first + 1, fresh_b, turned_b)):
            pass
        following = jnp.minimum(first + 2, DIRS - 1)
        for _ in zip(finish(first + 1, from_west, fresh_b, turned_b),
                     prepare(following, fresh_a, turned_a)):
            pass
        departure(pair).start()

    for from_west in (True, False):
        start = 0 if from_west else PAIRS // 2
        lax.fori_loop(start, start + PAIRS // 2,
                      lambda pair, carry: (two_directions(from_west, pair), carry)[1], 0)
    for pair in range(PAIRS):
        departure(pair).wait()


def advect(action, courant, wet, west, east, south, north):
    fresh = pltpu.VMEM((FREQS, LANES), f32)
    turned = pltpu.VMEM((FREQS * TILE_X, LANES), bf16)
    return pl.pallas_call(
        advect_kernel,
        in_specs=[HBM_SPACE] * 7,
        out_specs=HBM_SPACE,
        out_shape=jax.ShapeDtypeStruct(action.shape, bf16),
        scratch_shapes=[pltpu.SMEM((FREQS,), f32), pltpu.SMEM((DIRS * 2,), f32),
                        pltpu.VMEM((TILE_X, LANES), jnp.int32),
                        pltpu.VMEM((HALF_ROWS, LANES), bf16), pltpu.VMEM((HALF_ROWS, LANES), bf16),
                        pltpu.VMEM((COLUMN_ROWS, LANES), bf16),
                        pltpu.VMEM((COLUMN_ROWS, LANES), bf16),
                        pltpu.VMEM(action.shape, bf16), pltpu.VMEM(action.shape, bf16),
                        fresh, fresh, turned, turned,
                        pltpu.SemaphoreType.DMA((PAIRS,)), pltpu.SemaphoreType.DMA((6,)),
                        pltpu.SemaphoreType.DMA((PAIRS,))],
        compiler_params=pltpu.CompilerParams(vmem_limit_bytes=MIDDLE),
        cost_estimate=pl.CostEstimate(
            flops=5 * 10**7, bytes_accessed=19 * 10**6, transcendentals=0),
        name="advect",
    )(courant, action, wet, west, east, south, north)


OCEAN_BLOCK = 5


def ocean_kernel(profile, stress, regrid, wet_int, velocity, tracer,
                 behind, ahead, velocity_hbm, tracer_hbm, velocity_next, tracer_next, force, left):
    shape = (SEGMENTS, LANES)
    lane = lax.broadcasted_iota(jnp.int32, shape, 1)
    segment = lax.broadcasted_iota(jnp.int32, shape, 0)

    def north_of(cells):
        turned = pltpu.roll(cells, LANES - 1, 1)
        following = jnp.where(segment == SEGMENTS - 1, 0.0, pltpu.roll(turned, SEGMENTS - 1, 0))
        return jnp.where(lane == LANES - 1, following, turned)

    def south_of(cells):
        turned = pltpu.roll(cells, 1, 1)
        preceding = jnp.where(segment == 0, 0.0, pltpu.roll(turned, 1, 0))
        return jnp.where(lane == 0, preceding, turned)

    at_end = (lax.axis_index("gx") == lax.axis_size("gx") - 1) & (
        lax.axis_index("gy") == lax.axis_size("gy") - 1)

    if True:
        def stress_row(part, row):
            return stress[pl.ds(part * 5 + row + 1, SEGMENTS, stride=16), :]

        def wave_force(first, second, row):
            across = stress_row(second, row)
            return -((stress_row(first, row + 1) - stress_row(first, row - 1)) / 2.0
                     + (north_of(across) - south_of(across)) / 2.0)

        for part in range(2):
            lines = [wave_force(part, part + 1, row) for row in range(3)]
            lines[2] = jnp.where(at_end, 0.0, lines[2])
            shifted = [north_of(cells) for cells in lines]
            for row in range(2):
                fraction = [
                    regrid[corner, pl.ds(row, SEGMENTS, stride=2), :].astype(f32) / 65536.0
                    for corner in range(4)]
                force[part, row] = (
                    fraction[0] * lines[row] + fraction[1] * shifted[row]
                    + fraction[2] * lines[row + 1] + fraction[3] * shifted[row + 1])

    wet = [wet_int[pl.ds(row, SEGMENTS, stride=2), :].astype(f32) for row in range(2)]

    def level_step(index):
        weight = profile[index]

        def around(source, field, place):
            first = source[field, index, pl.ds(0, SEGMENTS, stride=2), :]
            last = source[field, index, pl.ds(1, SEGMENTS, stride=2), :]
            at = pl.ds(pl.multiple_of((index * 4 + place) * SEGMENTS, SEGMENTS), SEGMENTS)
            west = behind[at, :].astype(f32)
            east = ahead[at, :].astype(f32)
            return ((first, west, last, south_of(first), north_of(first)),
                    (last, first, east, south_of(last), north_of(last)))

        zonal, meridional = around(velocity, 0, 0), around(velocity, 1, 1)
        fresh, old = around(tracer, 0, 2), around(tracer, 1, 3)
        for row in range(2):
            def spread(field):
                center, west, east, south, north = field[row]
                return center + VISCOSITY * (west + east + south + north - 4.0 * center)

            u, v = zonal[row][0], meridional[row][0]
            u_next = wet[row] * (spread(zonal) + CORIOLIS * v + weight * force[0, row])
            v_next = wet[row] * (spread(meridional) - CORIOLIS * u + weight * force[1, row])
            speed_x = jnp.clip(u_next, -COURANT_MAX, COURANT_MAX)
            speed_y = jnp.clip(v_next, -COURANT_MAX, COURANT_MAX)
            forward_x, backward_x = jnp.maximum(speed_x, 0.0), jnp.minimum(speed_x, 0.0)
            forward_y, backward_y = jnp.maximum(speed_y, 0.0), jnp.minimum(speed_y, 0.0)

            def upwind(field):
                center, west, east, south, north = field[row]
                return (center - forward_x * (center - west) - backward_x * (east - center)
                        - forward_y * (center - south) - backward_y * (north - center))

            at = pl.ds(row, SEGMENTS, stride=2)
            velocity_next[0, index, at, :] = u_next
            velocity_next[1, index, at, :] = v_next
            tracer_next[0, index, at, :] = wet[row] * upwind(fresh)
            tracer_next[1, index, at, :] = wet[row] * (upwind(old) + AGE_RATE * fresh[row][0])

    def departures(step):
        levels = pl.ds(step * OCEAN_BLOCK, OCEAN_BLOCK)
        return [pltpu.make_async_copy(source.at[:, levels], target.at[:, levels],
                                      left.at[order, step])
                for order, (source, target) in enumerate(
                    ((velocity_next, velocity_hbm), (tracer_next, tracer_hbm)))]

    def block(step, carry):
        for sub in range(OCEAN_BLOCK):
            level_step(step * OCEAN_BLOCK + sub)
        for copy in departures(step):
            copy.start()
        return carry

    lax.fori_loop(0, LEVELS // OCEAN_BLOCK, block, 0)
    for step in range(LEVELS // OCEAN_BLOCK):
        for copy in departures(step):
            copy.wait()


def ocean(profile, stress, regrid, wet, velocity, tracer, behind, ahead):
    return pl.pallas_call(
        ocean_kernel,
        in_specs=[SMEM_SPACE] + [VMEM_SPACE] * 7,
        out_specs=[HBM_SPACE] * 2,
        out_shape=[jax.ShapeDtypeStruct(velocity.shape, f32)] * 2,
        scratch_shapes=[pltpu.VMEM(velocity.shape, f32), pltpu.VMEM(tracer.shape, f32),
                        pltpu.VMEM((2, 2, SEGMENTS, LANES), f32),
                        pltpu.SemaphoreType.DMA((2, LEVELS // OCEAN_BLOCK))],
        compiler_params=pltpu.CompilerParams(vmem_limit_bytes=VMEM),
        cost_estimate=pl.CostEstimate(
            flops=2 * 10**7, bytes_accessed=4 * 10**6, transcendentals=0),
        name="ocean",
    )(profile, stress, regrid, wet, velocity, tracer, behind, ahead)


def to_segments(cells):
    lead = cells.shape[:-2]
    split = cells.reshape(lead + (2, SEGMENTS, LANES))
    return jnp.swapaxes(split, -3, -2).reshape(lead + (2 * SEGMENTS, LANES))


def from_segments(cells):
    lead = cells.shape[:-2]
    split = cells.reshape(lead + (SEGMENTS, 2, LANES))
    return jnp.swapaxes(split, -3, -2).reshape(lead + (2, SEGMENTS * LANES))


def shift(block, axes, distance):
    count = lax.axis_size(axes)
    return lax.ppermute(
        block, axes,
        [(i, i + distance) for i in range(count) if 0 <= i + distance < count])


def local(action, courant, freq_weight, wave_wet, regrid_weights, velocity, tracer, profile,
          ocean_wet):
    ring = ("gx", "gy")
    flow, mass = to_segments(velocity), to_segments(tracer)
    stress, to_east, to_west, early = gather(action, freq_weight)
    west = shift(to_east, "gx", 1)
    east = shift(to_west, "gx", -1)
    to_north, to_south = edge_columns(action, flow, mass, early)
    to_north, to_south, west, east = lax.optimization_barrier(
        (to_north, to_south, west, east))
    behind = shift(to_north, ring, 1)
    ahead = shift(to_south, ring, -1)
    strips = lax.all_to_all(
        pack(stress, west, east).reshape(SEGMENTS, 16, LANES), "gy",
        split_axis=0, concat_axis=0, tiled=True).reshape(2 * LANES, LANES)
    action_next = advect(
        action, courant, wave_wet, west, east, behind, ahead)
    flow_next, mass_next = ocean(
        profile, strips, to_segments(regrid_weights), to_segments(ocean_wet),
        flow, mass, behind, ahead)
    return action_next, from_segments(flow_next), from_segments(mass_next)


def solution(mesh):
    return jax.shard_map(
        local,
        mesh=mesh,
        in_specs=(
            P(None, None, "gx", "gy"),
            P(),
            P(),
            P("gx", "gy"),
            P(None, ("gx", "gy"), None),
            P(None, None, ("gx", "gy"), None),
            P(None, None, ("gx", "gy"), None),
            P(),
            P(("gx", "gy"), None),
        ),
        out_specs=(
            P(None, None, "gx", "gy"),
            P(None, None, ("gx", "gy"), None),
            P(None, None, ("gx", "gy"), None),
        ),
        check_vma=False,
    )
```

```python
import functools

import jax
import jax.numpy as jnp
import numpy as np
from jax import lax
from jax.experimental import pallas as pl
from jax.experimental.pallas import tpu as pltpu
from jax.sharding import PartitionSpec as P

VISCOSITY = 0.1
CORIOLIS = 0.25
COURANT_MAX = 0.4
AGE_RATE = 0.5

DIRS = 36
FREQS = 32
GROUP = 3
STEPS = DIRS // GROUP
QUARTER = STEPS // 4
TILE_X = 32
LANES = 128
LEVELS = 20
SEGMENTS = 16
EDGE_ROWS = 4 * LEVELS * SEGMENTS
COLUMN_ROWS = (STEPS // 2) * TILE_X
RING_ROWS = EDGE_ROWS + COLUMN_ROWS
HALF_ROWS = DIRS // 2 * FREQS
RIM = 16
ROW_ROWS = HALF_ROWS + 3 * RIM
VMEM = 28 * 2**20
MIDDLE = 48 * 2**20
WIDE = 56 * 2**20

f32 = jnp.float32
bf16 = jnp.bfloat16


def direction_table():
    angles = -np.pi / 2 + 2.0 * np.pi * (np.arange(DIRS) + 0.5) / DIRS
    cosine, sine = np.cos(angles), np.sin(angles)
    return np.stack(
        [cosine * cosine / DIRS, cosine * sine / DIRS, sine * sine / DIRS,
         np.abs(cosine), np.abs(sine)], axis=1).astype(np.float32)


def write_table(table, columns):
    for angle, values in enumerate(direction_table()):
        for place, column in enumerate(columns):
            table[angle * len(columns) + place] = f32(values[column])


def from_west(quarter):
    return quarter < 2


def from_south(quarter):
    return quarter in (1, 2)


def column_slot(quarter, step):
    if from_south(quarter):
        return step - QUARTER
    return step if quarter == 0 else step - 2 * QUARTER


def thirds(values):
    high = values.astype(bf16)
    rest = values - high.astype(f32)
    middle = rest.astype(bf16)
    return high, middle, (rest - middle.astype(f32)).astype(bf16)


def write_one_hot(one_hot):
    lane = lax.broadcasted_iota(jnp.int32, (16, LANES), 1)
    for place in range(GROUP * FREQS):
        one_hot[pl.ds(place * 16, 16), :] = jnp.where(lane == place, 1.0, 0.0).astype(bf16)


def no_columns():
    return (jnp.zeros((16, LANES), bf16),) * 8


def add_column(columns, tile, one_hot, index, freq, turn):
    place = index * FREQS + freq
    hot = one_hot[pl.ds(pl.multiple_of(place * 16, 16), 16), :]
    rolled = pltpu.roll(tile, place + turn, 1)
    for half in range(2):
        part = freq % 4 * 2 + half
        columns[part] = columns[part] + rolled[half * 16:half * 16 + 16] * hot


def put_columns(target, first, columns):
    at = pl.multiple_of(first, TILE_X)
    for half in range(2):
        target[pl.ds(at + half * 16, 16), :] = (
            (columns[half] + columns[2 + half]) + (columns[4 + half] + columns[6 + half]))


def gather_kernel(weight_hbm, action_hbm, stress, to_east, to_west, early,
                  weight, table, action, one_hot, picked, rim, arrived, others):
    def arrival(step):
        slab = pl.ds(step * GROUP, GROUP)
        return pltpu.make_async_copy(action_hbm.at[slab], action.at[slab], arrived.at[step])

    weights_arrive = pltpu.make_async_copy(weight_hbm, weight, others.at[0])
    weights_arrive.start()
    for step in range(STEPS):
        arrival(step).start()
    write_table(table, (0, 1, 2))
    write_one_hot(one_hot)
    stress[...] = jnp.zeros_like(stress)
    weights_arrive.wait()

    def sweep(west_side, step):
        tile, row = (1, 15) if west_side else (0, 0)
        rows, first_step = (to_east, 0) if west_side else (to_west, STEPS // 2)
        turn = jnp.where(step < QUARTER, 0, 1)
        arrival(step).wait()

        def direction(index, columns):
            angle = step * GROUP + index
            energy = [jnp.zeros((16, LANES), f32)] * 4
            columns = list(columns)
            for freq in range(FREQS):
                if west_side:
                    add_column(columns, action[angle, freq], one_hot, index, freq, turn)
                for half in range(2):
                    own = action[angle, freq, pl.ds(half * 16, 16), :].astype(f32)
                    part = freq % 2 * 2 + half
                    energy[part] = energy[part] + weight[freq] * own
                    if half == tile:
                        picked[freq:freq + 1, :] = own[row:row + 1, :]
            at = (step - first_step) * (GROUP * FREQS) + index * FREQS
            rows[pl.ds(pl.multiple_of(at, FREQS), FREQS), :] = picked[...].astype(bf16)
            for half in range(2):
                both = energy[half] + energy[2 + half]
                for part in range(3):
                    stress[part, pl.ds(half * 16, 16), :] += table[angle * 3 + part] * both
            return tuple(columns)

        columns = lax.fori_loop(0, GROUP, direction, no_columns() if west_side else ())
        if west_side:
            put_columns(early, step * TILE_X, columns)

    for west_side in (True, False):
        start = 0 if west_side else STEPS // 2
        lax.fori_loop(start, start + STEPS // 2,
                      lambda step, carry: (sweep(west_side, step), carry)[1], 0)

    for target, lines in ((to_east, (TILE_X - 1,)), (to_west, (0, 1))):
        rim[...] = jnp.zeros_like(rim)
        for part in range(3):
            for order, line in enumerate(lines):
                rim[part * 2 + order:part * 2 + order + 1, :] = stress[part, line:line + 1, :]
        for order, piece in enumerate(thirds(rim[...])):
            target[pl.ds(HALF_ROWS + order * RIM, RIM), :] = piece


VMEM_SPACE = pl.BlockSpec(memory_space=pltpu.VMEM)
SMEM_SPACE = pl.BlockSpec(memory_space=pltpu.SMEM)
HBM_SPACE = pl.BlockSpec(memory_space=pltpu.HBM)


def gather(action, weight):
    return pl.pallas_call(
        gather_kernel,
        in_specs=[HBM_SPACE] * 2,
        out_specs=[VMEM_SPACE] * 4,
        out_shape=[jax.ShapeDtypeStruct((3, TILE_X, LANES), f32)]
        + [jax.ShapeDtypeStruct((ROW_ROWS, LANES), bf16)] * 2
        + [jax.ShapeDtypeStruct((COLUMN_ROWS, LANES), bf16)],
        scratch_shapes=[pltpu.SMEM((FREQS,), f32), pltpu.SMEM((DIRS * 3,), f32),
                        pltpu.VMEM(action.shape, bf16),
                        pltpu.VMEM((GROUP * FREQS * 16, LANES), bf16),
                        pltpu.VMEM((FREQS, LANES), f32),
                        pltpu.VMEM((RIM, LANES), f32),
                        pltpu.SemaphoreType.DMA((STEPS,)), pltpu.SemaphoreType.DMA((1,))],
        compiler_params=pltpu.CompilerParams(vmem_limit_bytes=WIDE),
        cost_estimate=pl.CostEstimate(
            flops=10**7, bytes_accessed=10**7, transcendentals=0),
        name="stress_and_rows",
    )(weight, action)


def columns_kernel(action_hbm, velocity_hbm, tracer_hbm, early_hbm, to_north, to_south,
                   action, velocity, tracer, one_hot, arrived, others):
    half_steps, half_columns = STEPS // 2, COLUMN_ROWS // 2

    def arrival(step):
        return pltpu.make_async_copy(
            action_hbm.at[pl.ds(step * GROUP, GROUP)],
            action.at[pl.ds((step - half_steps) * GROUP, GROUP)], arrived.at[step - half_steps])

    strips = [pltpu.make_async_copy(source, target, others.at[order])
              for order, (source, target) in enumerate((
                  (velocity_hbm, velocity), (tracer_hbm, tracer),
                  (early_hbm.at[pl.ds(0, half_columns)],
                   to_south.at[pl.ds(EDGE_ROWS, half_columns)]),
                  (early_hbm.at[pl.ds(half_columns, half_columns)],
                   to_north.at[pl.ds(EDGE_ROWS, half_columns)])))]
    for step in range(half_steps, STEPS):
        arrival(step).start()
    for copy in strips:
        copy.start()
    write_one_hot(one_hot)

    def sweep(quarter, step):
        turn = 1 if from_south(quarter) else 0
        arrival(step).wait()

        def direction(index, columns):
            columns = list(columns)
            angle = (step - half_steps) * GROUP + index
            for freq in range(FREQS):
                add_column(columns, action[angle, freq], one_hot, index, freq, turn)
            return tuple(columns)

        columns = lax.fori_loop(0, GROUP, direction, no_columns())
        put_columns(to_north if from_south(quarter) else to_south,
                    EDGE_ROWS + column_slot(quarter, step) * TILE_X, columns)

    for quarter in (2, 3):
        lax.fori_loop(quarter * QUARTER, (quarter + 1) * QUARTER,
                      lambda step, carry: (sweep(quarter, step), carry)[1], 0)

    for pair, source in enumerate((velocity, tracer)):
        strips[pair].wait()

        def edges(level, carry):
            for field in range(2):
                place = (level * 4 + pair * 2 + field) * SEGMENTS
                at = pl.ds(pl.multiple_of(place, SEGMENTS), SEGMENTS)
                to_south[at, :] = source[field, level, pl.ds(0, SEGMENTS, stride=2), :].astype(bf16)
                to_north[at, :] = source[field, level, pl.ds(1, SEGMENTS, stride=2), :].astype(bf16)
            return carry

        lax.fori_loop(0, LEVELS, edges, 0, unroll=5)
    strips[2].wait()
    strips[3].wait()


def edge_columns(action, velocity, tracer, early):
    return pl.pallas_call(
        columns_kernel,
        in_specs=[HBM_SPACE] * 4,
        out_specs=[VMEM_SPACE] * 2,
        out_shape=[jax.ShapeDtypeStruct((RING_ROWS, LANES), bf16)] * 2,
        scratch_shapes=[pltpu.VMEM((DIRS // 2,) + action.shape[1:], bf16),
                        pltpu.VMEM(velocity.shape, f32),
                        pltpu.VMEM(tracer.shape, f32),
                        pltpu.VMEM((GROUP * FREQS * 16, LANES), bf16),
                        pltpu.SemaphoreType.DMA((STEPS // 2,)), pltpu.SemaphoreType.DMA((4,))],
        compiler_params=pltpu.CompilerParams(vmem_limit_bytes=WIDE),
        cost_estimate=pl.CostEstimate(
            flops=10**7, bytes_accessed=7 * 10**6, transcendentals=0),
        name="ring_edges",
    )(action, velocity, tracer, early)


def pack_kernel(stress, west, east, packed, tall):
    def rim(source):
        pieces = [source[pl.ds(order * RIM, RIM), :].astype(f32) for order in range(3)]
        return pieces[0] + pieces[1] + pieces[2]

    before, after = rim(west), rim(east)
    for part in range(3):
        tall[part, pl.ds(8, TILE_X), :] = stress[part]
        tall[part, 7:8, :] = before[part * 2:part * 2 + 1, :]
        tall[part, 8 + TILE_X:10 + TILE_X, :] = after[part * 2:part * 2 + 2, :]
        for order in range(5):
            packed[pl.ds(part * 5 + order, SEGMENTS, stride=16), :] = (
                tall[part, pl.ds(7 + order, SEGMENTS, stride=2), :])
    packed[pl.ds(15, SEGMENTS, stride=16), :] = jnp.zeros((SEGMENTS, LANES), f32)


def pack(stress, west, east):
    tail = pl.BlockSpec((3 * RIM, LANES), lambda i: (HALF_ROWS // (3 * RIM), 0))
    return pl.pallas_call(
        pack_kernel,
        grid=(1,),
        in_specs=[pl.BlockSpec((3, TILE_X, LANES), lambda i: (0, 0, 0)), tail, tail],
        out_specs=pl.BlockSpec((2 * LANES, LANES), lambda i: (0, 0)),
        out_shape=jax.ShapeDtypeStruct((2 * LANES, LANES), f32),
        scratch_shapes=[pltpu.VMEM((3, 48, LANES), f32)],
        compiler_params=pltpu.CompilerParams(vmem_limit_bytes=VMEM),
        name="pack",
    )(stress, west, east)


HALVES = (0, 16)
PAIRS = DIRS // 2


def advect_kernel(courant_hbm, action_hbm, wet_hbm, west_hbm, east_hbm, south_hbm, north_hbm,
                  moved_hbm, courant, table, wet_int, west, east, south, north,
                  action, moved, fresh_a, fresh_b, turned_a, turned_b, arrived, others, left):
    lane = lax.broadcasted_iota(jnp.int32, (TILE_X, LANES), 1)
    line = lax.broadcasted_iota(jnp.int32, (8, LANES), 0)
    at_y, count_y = lax.axis_index("gy"), lax.axis_size("gy")

    def arrival(pair):
        slab = pl.ds(pair * 2, 2)
        return pltpu.make_async_copy(action_hbm.at[slab], action.at[slab], arrived.at[pair])

    def departure(pair):
        slab = pl.ds(pair * 2, 2)
        return pltpu.make_async_copy(moved.at[slab], moved_hbm.at[slab], left.at[pair])

    columns = pl.ds(EDGE_ROWS, COLUMN_ROWS)
    halos = [pltpu.make_async_copy(source, target, others.at[order])
             for order, (source, target) in enumerate((
                 (courant_hbm, courant), (wet_hbm, wet_int),
                 (west_hbm.at[pl.ds(0, HALF_ROWS)], west), (east_hbm.at[pl.ds(0, HALF_ROWS)], east),
                 (south_hbm.at[columns], south), (north_hbm.at[columns], north)))]
    arrival(0).start()
    for copy in halos:
        copy.start()
    for pair in range(1, PAIRS):
        arrival(pair).start()
    write_table(table, (3, 4))
    for copy in halos:
        copy.wait()
    wet = [wet_int[pl.ds(half, 16), :].astype(f32).astype(bf16) for half in HALVES]

    def prepare(angle, fresh, turned):
        westward = angle >= DIRS // 2
        southern = (angle >= DIRS // 4) & (angle < 3 * DIRS // 4)
        step = angle // GROUP
        near = pl.ds(pl.multiple_of(
            jnp.where(westward, angle - DIRS // 2, angle) * FREQS, FREQS), FREQS)
        fresh[...] = jnp.where(westward, east[near, :].astype(f32), west[near, :].astype(f32))
        slot = jnp.where(southern, step - QUARTER,
                         jnp.where(step < QUARTER, step, step - 2 * QUARTER))
        at = pl.ds(pl.multiple_of(slot * TILE_X, TILE_X), TILE_X)
        inside = jnp.where(southern, at_y > 0, at_y < count_y - 1).astype(f32)
        column = (jnp.where(southern, south[at, :].astype(f32), north[at, :].astype(f32))
                  * inside).astype(bf16)
        turn = jnp.where(southern, 1, LANES - 1)
        target = jnp.where(southern, LANES, 2 * LANES - 1) - (angle - step * GROUP) * FREQS
        empty = lane == jnp.where(southern, 0, LANES - 1)
        for freq in range(FREQS):
            own = action[angle, freq]
            turned[pl.ds(freq * TILE_X, TILE_X), :] = jnp.where(
                empty, pltpu.roll(column, target - freq, 1), pltpu.roll(own, turn, 1))
            yield

    def finish(angle, from_west, fresh, turned):
        size_x, size_y = table[angle * 2], table[angle * 2 + 1]
        edge = line == (0 if from_west else 7)
        for freq in range(FREQS):
            speed_x = courant[freq] * size_x
            speed_y = courant[freq] * size_y
            stay = 1.0 - speed_x - speed_y
            own = action[angle, freq].astype(f32)
            turned_rows = [pltpu.roll(own[first:first + 8], 1 if from_west else 7, 0)
                           for first in range(0, TILE_X, 8)]
            halo = jnp.broadcast_to(fresh[freq:freq + 1, :], (8, LANES))
            entering = ([halo] + turned_rows[:-1] if from_west else turned_rows[1:] + [halo])
            along_x = jnp.concatenate(
                [jnp.where(edge, incoming, rows)
                 for incoming, rows in zip(entering, turned_rows)], axis=0)
            along_y = turned[pl.ds(freq * TILE_X, TILE_X), :].astype(f32)
            result = (stay * own + speed_x * along_x + speed_y * along_y).astype(bf16)
            for order, half in enumerate(HALVES):
                moved[angle, freq, pl.ds(half, 16), :] = result[half:half + 16] * wet[order]
            yield

    arrival(0).wait()
    for _ in prepare(jnp.int32(0), fresh_a, turned_a):
        pass

    def two_directions(from_west, pair):
        @pl.when(pair < PAIRS - 1)
        def _():
            arrival(pair + 1).wait()

        first = pair * 2
        for _ in zip(finish(first, from_west, fresh_a, turned_a),
                     prepare(first + 1, fresh_b, turned_b)):
            pass
        following = jnp.minimum(first + 2, DIRS - 1)
        for _ in zip(finish(first + 1, from_west, fresh_b, turned_b),
                     prepare(following, fresh_a, turned_a)):
            pass
        departure(pair).start()

    for from_west in (True, False):
        start = 0 if from_west else PAIRS // 2
        lax.fori_loop(start, start + PAIRS // 2,
                      lambda pair, carry: (two_directions(from_west, pair), carry)[1], 0)
    for pair in range(PAIRS):
        departure(pair).wait()


def advect(action, courant, wet, west, east, south, north):
    fresh = pltpu.VMEM((FREQS, LANES), f32)
    turned = pltpu.VMEM((FREQS * TILE_X, LANES), bf16)
    return pl.pallas_call(
        advect_kernel,
        in_specs=[HBM_SPACE] * 7,
        out_specs=HBM_SPACE,
        out_shape=jax.ShapeDtypeStruct(action.shape, bf16),
        scratch_shapes=[pltpu.SMEM((FREQS,), f32), pltpu.SMEM((DIRS * 2,), f32),
                        pltpu.VMEM((TILE_X, LANES), jnp.int32),
                        pltpu.VMEM((HALF_ROWS, LANES), bf16), pltpu.VMEM((HALF_ROWS, LANES), bf16),
                        pltpu.VMEM((COLUMN_ROWS, LANES), bf16),
                        pltpu.VMEM((COLUMN_ROWS, LANES), bf16),
                        pltpu.VMEM(action.shape, bf16), pltpu.VMEM(action.shape, bf16),
                        fresh, fresh, turned, turned,
                        pltpu.SemaphoreType.DMA((PAIRS,)), pltpu.SemaphoreType.DMA((6,)),
                        pltpu.SemaphoreType.DMA((PAIRS,))],
        compiler_params=pltpu.CompilerParams(vmem_limit_bytes=MIDDLE),
        cost_estimate=pl.CostEstimate(
            flops=5 * 10**7, bytes_accessed=19 * 10**6, transcendentals=0),
        name="advect",
    )(courant, action, wet, west, east, south, north)


OCEAN_BLOCK = 5


def ocean_kernel(profile, stress, regrid, wet_int, velocity, tracer,
                 behind, ahead, velocity_hbm, tracer_hbm, velocity_next, tracer_next, force, left):
    shape = (SEGMENTS, LANES)
    lane = lax.broadcasted_iota(jnp.int32, shape, 1)
    segment = lax.broadcasted_iota(jnp.int32, shape, 0)

    def north_of(cells):
        turned = pltpu.roll(cells, LANES - 1, 1)
        following = jnp.where(segment == SEGMENTS - 1, 0.0, pltpu.roll(turned, SEGMENTS - 1, 0))
        return jnp.where(lane == LANES - 1, following, turned)

    def south_of(cells):
        turned = pltpu.roll(cells, 1, 1)
        preceding = jnp.where(segment == 0, 0.0, pltpu.roll(turned, 1, 0))
        return jnp.where(lane == 0, preceding, turned)

    at_end = (lax.axis_index("gx") == lax.axis_size("gx") - 1) & (
        lax.axis_index("gy") == lax.axis_size("gy") - 1)

    if True:
        def stress_row(part, row):
            return stress[pl.ds(part * 5 + row + 1, SEGMENTS, stride=16), :]

        def wave_force(first, second, row):
            across = stress_row(second, row)
            return -((stress_row(first, row + 1) - stress_row(first, row - 1)) / 2.0
                     + (north_of(across) - south_of(across)) / 2.0)

        for part in range(2):
            lines = [wave_force(part, part + 1, row) for row in range(3)]
            lines[2] = jnp.where(at_end, 0.0, lines[2])
            shifted = [north_of(cells) for cells in lines]
            for row in range(2):
                fraction = [
                    regrid[corner, pl.ds(row, SEGMENTS, stride=2), :].astype(f32) / 65536.0
                    for corner in range(4)]
                force[part, row] = (
                    fraction[0] * lines[row] + fraction[1] * shifted[row]
                    + fraction[2] * lines[row + 1] + fraction[3] * shifted[row + 1])

    wet = [wet_int[pl.ds(row, SEGMENTS, stride=2), :].astype(f32) for row in range(2)]

    def level_step(index):
        weight = profile[index]

        def around(source, field, place):
            first = source[field, index, pl.ds(0, SEGMENTS, stride=2), :]
            last = source[field, index, pl.ds(1, SEGMENTS, stride=2), :]
            at = pl.ds(pl.multiple_of((index * 4 + place) * SEGMENTS, SEGMENTS), SEGMENTS)
            west = behind[at, :].astype(f32)
            east = ahead[at, :].astype(f32)
            return ((first, west, last, south_of(first), north_of(first)),
                    (last, first, east, south_of(last), north_of(last)))

        zonal, meridional = around(velocity, 0, 0), around(velocity, 1, 1)
        fresh, old = around(tracer, 0, 2), around(tracer, 1, 3)
        for row in range(2):
            def spread(field):
                center, west, east, south, north = field[row]
                return center + VISCOSITY * (west + east + south + north - 4.0 * center)

            u, v = zonal[row][0], meridional[row][0]
            u_next = wet[row] * (spread(zonal) + CORIOLIS * v + weight * force[0, row])
            v_next = wet[row] * (spread(meridional) - CORIOLIS * u + weight * force[1, row])
            speed_x = jnp.clip(u_next, -COURANT_MAX, COURANT_MAX)
            speed_y = jnp.clip(v_next, -COURANT_MAX, COURANT_MAX)
            forward_x, backward_x = jnp.maximum(speed_x, 0.0), jnp.minimum(speed_x, 0.0)
            forward_y, backward_y = jnp.maximum(speed_y, 0.0), jnp.minimum(speed_y, 0.0)

            def upwind(field):
                center, west, east, south, north = field[row]
                return (center - forward_x * (center - west) - backward_x * (east - center)
                        - forward_y * (center - south) - backward_y * (north - center))

            at = pl.ds(row, SEGMENTS, stride=2)
            velocity_next[0, index, at, :] = u_next
            velocity_next[1, index, at, :] = v_next
            tracer_next[0, index, at, :] = wet[row] * upwind(fresh)
            tracer_next[1, index, at, :] = wet[row] * (upwind(old) + AGE_RATE * fresh[row][0])

    def departures(step):
        levels = pl.ds(step * OCEAN_BLOCK, OCEAN_BLOCK)
        return [pltpu.make_async_copy(source.at[:, levels], target.at[:, levels],
                                      left.at[order, step])
                for order, (source, target) in enumerate(
                    ((velocity_next, velocity_hbm), (tracer_next, tracer_hbm)))]

    def block(step, carry):
        for sub in range(OCEAN_BLOCK):
            level_step(step * OCEAN_BLOCK + sub)
        for copy in departures(step):
            copy.start()
        return carry

    lax.fori_loop(0, LEVELS // OCEAN_BLOCK, block, 0)
    for step in range(LEVELS // OCEAN_BLOCK):
        for copy in departures(step):
            copy.wait()


def ocean(profile, stress, regrid, wet, velocity, tracer, behind, ahead):
    return pl.pallas_call(
        ocean_kernel,
        in_specs=[SMEM_SPACE] + [VMEM_SPACE] * 7,
        out_specs=[HBM_SPACE] * 2,
        out_shape=[jax.ShapeDtypeStruct(velocity.shape, f32)] * 2,
        scratch_shapes=[pltpu.VMEM(velocity.shape, f32), pltpu.VMEM(tracer.shape, f32),
                        pltpu.VMEM((2, 2, SEGMENTS, LANES), f32),
                        pltpu.SemaphoreType.DMA((2, LEVELS // OCEAN_BLOCK))],
        compiler_params=pltpu.CompilerParams(vmem_limit_bytes=VMEM),
        cost_estimate=pl.CostEstimate(
            flops=2 * 10**7, bytes_accessed=4 * 10**6, transcendentals=0),
        name="ocean",
    )(profile, stress, regrid, wet, velocity, tracer, behind, ahead)


def to_segments(cells):
    lead = cells.shape[:-2]
    split = cells.reshape(lead + (2, SEGMENTS, LANES))
    return jnp.swapaxes(split, -3, -2).reshape(lead + (2 * SEGMENTS, LANES))


def from_segments(cells):
    lead = cells.shape[:-2]
    split = cells.reshape(lead + (SEGMENTS, 2, LANES))
    return jnp.swapaxes(split, -3, -2).reshape(lead + (2, SEGMENTS * LANES))


def shift(block, axes, distance):
    count = lax.axis_size(axes)
    return lax.ppermute(
        block, axes,
        [(i, i + distance) for i in range(count) if 0 <= i + distance < count])


def local(action, courant, freq_weight, wave_wet, regrid_weights, velocity, tracer, profile,
          ocean_wet):
    ring = ("gx", "gy")
    flow, mass = to_segments(velocity), to_segments(tracer)
    stress, to_east, to_west, early = gather(action, freq_weight)
    west = shift(to_east, "gx", 1)
    east = shift(to_west, "gx", -1)
    to_north, to_south = edge_columns(action, flow, mass, early)
    to_north, to_south, west, east = lax.optimization_barrier(
        (to_north, to_south, west, east))
    behind = shift(to_north, ring, 1)
    ahead = shift(to_south, ring, -1)
    strips = lax.all_to_all(
        pack(stress, west, east).reshape(SEGMENTS, 16, LANES), "gy",
        split_axis=0, concat_axis=0, tiled=True).reshape(2 * LANES, LANES)
    action_next = advect(
        action, courant, wave_wet, west, east, behind, ahead)
    flow_next, mass_next = ocean(
        profile, strips, to_segments(regrid_weights), to_segments(ocean_wet),
        flow, mass, behind, ahead)
    return action_next, from_segments(flow_next), from_segments(mass_next)


def solution(mesh):
    return jax.shard_map(
        local,
        mesh=mesh,
        in_specs=(
            P(None, None, "gx", "gy"),
            P(),
            P(),
            P("gx", "gy"),
            P(None, ("gx", "gy"), None),
            P(None, None, ("gx", "gy"), None),
            P(None, None, ("gx", "gy"), None),
            P(),
            P(("gx", "gy"), None),
        ),
        out_specs=(
            P(None, None, "gx", "gy"),
            P(None, None, ("gx", "gy"), None),
            P(None, None, ("gx", "gy"), None),
        ),
        check_vma=False,
    )
```
